32 devices in a mesh: groups: 2 (over y), seq: 4 (over z), mp: 2 (over x), batch: 2 (over core).
Axes of the slice: x: 2, y: 2, z: 4, core: 2. Of those that a mesh axis runs over, the one named last changes fastest.
Arguments:
- image_token_states: bfloat16 [8, 576, 2432], P(('groups', 'batch'), 'seq'), parts along dimension 0, may hold values from -6 to 6
- timestep: int32 [8], P(('groups', 'batch')), parts along dimension 0, may hold values from 0 to 9
- prompt_token_length: int32 [8], P(('groups', 'batch')), parts along dimension 0, may hold values from 1 to 84, as said below
- modulation: float32 [10, 3, 2432], replicated, may hold values from -3 to 11
- text_key_value: bfloat16 [8, 2, 84, 1536], P(('groups', 'batch'), None, 'seq', 'mp'), parts along dimension 0, may hold values from -9 to 9
- frozen_query_key_value: bfloat16 [2432, 3, 1536], P(None, None, ('mp', 'batch')), may hold values from -0.125 to 0.125
- frozen_output_weight: bfloat16 [1536, 2432], P(('mp', 'batch')), may hold values from -0.15625 to 0.15625
- adapter_down_factors: bfloat16 [4, 32, 2432], P('seq'), may hold values from -0.125 to 0.125
- adapter_up_factors: bfloat16 [4, 32, 3, 1536], P('seq', None, None, 'mp'), may hold values from -1 to 1
- owner: int32 [3], replicated, may hold values from 0 to 3, as said below
Outputs:
- hidden_out: bfloat16 [8, 576, 2432], P(('groups', 'batch'), 'seq'), parts along dimension 0
The draws below stay inside these ranges and needn't reach their ends.
There are 2 independent parts, one for each index of `groups`. The reference program is written for one: setup_inputs(seed, part) draws one part's arguments, and reference() takes and returns one part's arrays. A program takes and returns all parts, laid end to end along the dimension named above; an argument that names none is the same for every part. Nothing has to cross between parts.
Inputs may be any that keep to these rules, and one draw needn't show every extreme that they name: `prompt_token_length`: in every draw some sample's prompt fills all 84 text slots. `owner`: the three entries are distinct.
All inputs are finite; a program needn't handle non-finite values.
Results may differ from the reference program's by a relative error of at most 0.012.
The reference program's roundings to bfloat16 on the way count: a program that leaves them out, or rounds other values in their place, can miss the bound.
Values may be sent and summed in bfloat16 or wider, within the bound.
A program may use at most 128 MiB of HBM per device.

```python
import jax
import jax.numpy as jnp
from jax import lax

MODEL_WIDTH = 2432
HEAD_SIZE = 64
H = 24
ADAPTER_RANK = 32
STEPS = 10
HEAD_FEATURES = 1536
IMG = 576
TXT = 84
SAMPLES = 4
N_SEQ = 4


def draw_prompt_token_length(key, part):
    key = jax.random.fold_in(key, 11)
    first, second = jax.random.split(key)
    lengths = jax.random.randint(first, (SAMPLES,), 1, TXT)
    picked = jax.random.randint(second, (), 0, SAMPLES)
    return jnp.where(jnp.arange(SAMPLES) == picked, TXT, lengths).astype(jnp.int32)


def draw_modulation(key, part):
    key = jax.random.fold_in(key, 23)
    key_shift, key_scale, key_gate = jax.random.split(key, 3)
    shift = jnp.clip(0.5 * jax.random.normal(key_shift, (STEPS, MODEL_WIDTH), jnp.float32), -3.0, 3.0)
    gate = jnp.clip(jax.random.normal(key_gate, (STEPS, MODEL_WIDTH), jnp.float32), -3.0, 3.0)
    scale = jax.random.uniform(key_scale, (STEPS, MODEL_WIDTH), jnp.float32, -0.5, 1.0)
    return jnp.stack([shift, scale, gate], axis=1).astype(jnp.float32)


def draw_owner(key, part):
    key = jax.random.fold_in(key, 37)
    first, second = jax.random.split(key)
    middle = jax.random.randint(first, (), 1, N_SEQ - 1)
    chosen = jnp.stack([jnp.int32(0), jnp.int32(N_SEQ - 1), middle.astype(jnp.int32)])
    return jax.random.permutation(second, chosen).astype(jnp.int32)


def with_ends(result, key, low, top_value):
    shape = result.shape
    place = [jax.random.randint(jax.random.fold_in(key, axis), (), 0, shape[axis]) for axis in range(len(shape))]
    result = result.at[tuple(place)].set(low)
    longest = shape.index(max(shape))
    place[longest] = (place[longest] + 1) % shape[longest]
    return result.at[tuple(place)].set(top_value)


def steps_of(own_key, dims, pieces, smallest, top_value):
    factor_of = 1.0
    for axis_at, shards_of in pieces:
        steps = jax.random.uniform(jax.random.fold_in(jax.random.fold_in(own_key, 6), axis_at), (shards_of,), jnp.float32, smallest / len(pieces), top_value / len(pieces))
        factor_of = factor_of * jnp.repeat(jnp.exp(steps), dims[axis_at] // shards_of).reshape((-1,) + (1,) * (len(dims) - 1 - axis_at))
    return factor_of


def gaussian(rng, extent, width, bound, shards=(), held_as=jnp.bfloat16):
    array = jax.random.normal(rng, extent, jnp.float32) * width
    if len(shards) > 0:
        array = steps_of(rng, extent, shards, -0.22, 0.18) * array
    return jnp.clip(array, min=-bound, max=bound).astype(held_as)


def setup_inputs(seed: int = 0, part: int = 0) -> dict:
    arg_keys = jax.random.split(jax.random.key(seed), 11)
    own_keys = jax.random.split(jax.random.fold_in(arg_keys[10], part), 11)
    image_token_states = gaussian(own_keys[0], (SAMPLES, IMG, MODEL_WIDTH), 1.0, 6.0, ((0, 2), (1, 4)))
    timestep = with_ends(jax.random.randint(own_keys[1], (SAMPLES,), 0, STEPS), jax.random.fold_in(own_keys[1], 1), 0, STEPS - 1).astype(jnp.int32)
    prompt_token_length = draw_prompt_token_length(jax.random.fold_in(jax.random.fold_in(arg_keys[10], part), 71), part)
    modulation = draw_modulation(jax.random.fold_in(arg_keys[10], 71), part)
    text_key_value = gaussian(own_keys[4], (SAMPLES, 2, TXT, HEAD_FEATURES), 3.0, 9.0, ((0, 2), (2, 4), (3, 2)))
    frozen_query_key_value = gaussian(arg_keys[5], (MODEL_WIDTH, 3, HEAD_FEATURES), MODEL_WIDTH ** -0.5, 0.125, ((2, 4),))
    frozen_output_weight = gaussian(arg_keys[6], (HEAD_FEATURES, MODEL_WIDTH), HEAD_FEATURES ** -0.5, 0.15625, ((0, 4),))
    adapter_down_factors = gaussian(arg_keys[7], (N_SEQ, ADAPTER_RANK, MODEL_WIDTH), MODEL_WIDTH ** -0.5, 0.125, ((0, 4),))
    adapter_up_factors = gaussian(arg_keys[8], (N_SEQ, ADAPTER_RANK, 3, HEAD_FEATURES), ADAPTER_RANK ** -0.5, 1.0, ((0, 4), (3, 2)))
    owner = draw_owner(jax.random.fold_in(arg_keys[10], 71), part)
    return {"image_token_states": image_token_states, "timestep": timestep, "prompt_token_length": prompt_token_length, "modulation": modulation, "text_key_value": text_key_value, "frozen_query_key_value": frozen_query_key_value, "frozen_output_weight": frozen_output_weight, "adapter_down_factors": adapter_down_factors, "adapter_up_factors": adapter_up_factors, "owner": owner}


def reference(image_token_states, timestep, prompt_token_length, modulation, text_key_value, frozen_query_key_value, frozen_output_weight, adapter_down_factors, adapter_up_factors, owner):
    mods = modulation[timestep]
    shift = mods[:, 0][:, None, :]
    scale = mods[:, 1][:, None, :]
    gate = mods[:, 2][:, None, :]
    wide = image_token_states.astype(jnp.float32)
    mean = lax.optimization_barrier(jnp.mean(wide, axis=-1, keepdims=True))
    centred = wide - mean
    var = lax.optimization_barrier(jnp.mean(centred * centred, axis=-1, keepdims=True))
    normed = (centred * lax.rsqrt(var + 1e-06) * (1.0 + scale) + shift).astype(jnp.bfloat16)
    down_factor = jnp.stack([adapter_down_factors[owner[0]], adapter_down_factors[owner[1]], adapter_down_factors[owner[2]]], axis=0).astype(jnp.float32)
    up_factor = jnp.stack([adapter_up_factors[owner[0]][:, 0], adapter_up_factors[owner[1]][:, 1], adapter_up_factors[owner[2]][:, 2]], axis=1).astype(jnp.float32)
    merged = (frozen_query_key_value.astype(jnp.float32) + jnp.einsum('crd,rcn->dcn', down_factor, up_factor)).astype(jnp.bfloat16)
    qkv = jnp.einsum('sid,dcn->sicn', normed.astype(jnp.float32), merged.astype(jnp.float32)).astype(jnp.bfloat16)
    queries = qkv[:, :, 0]
    keys = jnp.concatenate([qkv[:, :, 1], text_key_value[:, 0]], axis=1)
    values = jnp.concatenate([qkv[:, :, 2], text_key_value[:, 1]], axis=1)
    live_text = jnp.arange(TXT, dtype=jnp.int32)[None, :] < prompt_token_length[:, None]
    live = jnp.concatenate([jnp.ones((SAMPLES, IMG), dtype=bool), live_text], axis=1)
    query_heads = queries.reshape(SAMPLES, IMG, H, HEAD_SIZE).transpose(2, 0, 1, 3)
    key_heads = keys.reshape(SAMPLES, IMG + TXT, H, HEAD_SIZE).transpose(2, 0, 1, 3)
    value_heads = values.reshape(SAMPLES, IMG + TXT, H, HEAD_SIZE).transpose(2, 0, 1, 3)

    def one_head(operands):
        single_query, single_key, single_value = operands
        attention_scores = jnp.einsum('wlj,wcj->wlc', single_query.astype(jnp.float32), single_key.astype(jnp.float32)) * HEAD_SIZE ** (-0.5)
        attention_scores = jnp.where(live[:, None, :], attention_scores, -jnp.inf)
        top = lax.optimization_barrier(jnp.max(attention_scores, axis=-1, keepdims=True))
        expo = jnp.exp(attention_scores - top)
        total = lax.optimization_barrier(jnp.sum(expo, axis=-1, keepdims=True))
        attention_weights = expo.astype(jnp.bfloat16)
        reduced_sum = jnp.einsum('wmo,woh->wmh', attention_weights.astype(jnp.float32), single_value.astype(jnp.float32))
        return reduced_sum / total
    heads_out = lax.map(one_head, (query_heads, key_heads, value_heads))
    attn = heads_out.transpose(1, 2, 0, 3).reshape(SAMPLES, IMG, HEAD_FEATURES).astype(jnp.bfloat16)
    proj = jnp.einsum('sin,nd->sid', attn.astype(jnp.float32), frozen_output_weight.astype(jnp.float32))
    return (wide + gate * proj).astype(jnp.bfloat16)
```

```python
import jax
import jax.numpy as jnp
from jax import lax
from jax.sharding import PartitionSpec as P

HEAD_SIZE = 64


def broadcast(block, axis, source):
    block = jnp.where(lax.axis_index(axis) == source, block, jnp.zeros_like(block))
    return lax.psum(block, axis)


def body(
    image_token_states,
    timestep,
    prompt_token_length,
    modulation,
    text_key_value,
    frozen_query_key_value,
    frozen_output_weight,
    adapter_down_factors,
    adapter_up_factors,
    owner,
):
    samples, img_rows, width = image_token_states.shape
    txt_rows = text_key_value.shape[2]
    resident_columns = adapter_up_factors.shape[3]
    heads_here = resident_columns // HEAD_SIZE
    steps_all = modulation.shape[0]
    onehot = (timestep[:, None] == jnp.arange(steps_all, dtype=jnp.int32)[None, :]).astype(
        jnp.float32
    )
    mods = jnp.einsum("st,tcd->scd", onehot, modulation, precision=lax.Precision.HIGHEST)
    shift = mods[:, 0][:, None, :]
    scale = mods[:, 1][:, None, :]
    gate = mods[:, 2][:, None, :]
    wide = image_token_states.astype(jnp.float32)
    mean = jnp.mean(wide, axis=-1, keepdims=True)
    centred = wide - mean
    var = jnp.mean(centred * centred, axis=-1, keepdims=True)
    normed = (centred * lax.rsqrt(var + 1e-06) * (1.0 + scale) + shift).astype(jnp.bfloat16)
    down_list = []
    up_list = []
    for which in range(3):
        packed_tensor = jnp.concatenate(
            [adapter_down_factors[0], adapter_up_factors[0][:, which]], axis=1
        )
        packed_tensor = broadcast(packed_tensor, "seq", owner[which])
        down_list.append(packed_tensor[:, :width])
        up_list.append(packed_tensor[:, width:])
    down_factor = jnp.stack(down_list, axis=0)
    up_factor = jnp.stack(up_list, axis=1)
    delta = jnp.einsum("crd,rcn->dcn", down_factor, up_factor, preferred_element_type=jnp.float32)
    merged = (
        lax.all_gather(frozen_query_key_value, "batch", axis=2, tiled=True).astype(jnp.float32)
        + delta
    ).astype(jnp.bfloat16)
    qkv = jnp.einsum("sid,dcn->sicn", normed, merged, preferred_element_type=jnp.float32).astype(
        jnp.bfloat16
    )
    queries = qkv[:, :, 0]
    keys = jnp.concatenate([qkv[:, :, 1], text_key_value[:, 0]], axis=1)
    values = jnp.concatenate([qkv[:, :, 2], text_key_value[:, 1]], axis=1)
    query_heads = queries.reshape(samples, img_rows, heads_here, HEAD_SIZE)
    block = img_rows + txt_rows
    start_top = jnp.full((samples, heads_here, img_rows), -1e30, jnp.float32)
    top = start_top
    key_piece = lax.all_gather(keys, "seq", axis=1, tiled=True)
    value_piece = lax.all_gather(values, "seq", axis=1, tiled=True)
    count = key_piece.shape[1]
    position = jnp.arange(count, dtype=jnp.int32)
    shard = position // block
    inside = position % block
    text_index = shard * txt_rows + inside - img_rows
    live = (inside < img_rows)[None, :] | (text_index[None, :] < prompt_token_length[:, None])
    key_heads = key_piece.reshape(samples, count, heads_here, HEAD_SIZE)
    value_heads = value_piece.reshape(samples, count, heads_here, HEAD_SIZE)
    attention_scores = jnp.einsum(
        "sihe,snhe->shin", query_heads, key_heads, preferred_element_type=jnp.float32
    ) * HEAD_SIZE ** (-0.5)
    attention_scores = jnp.where(live[:, None, None, :], attention_scores, -1e30)
    new_top = jnp.maximum(top, jnp.max(attention_scores, axis=-1))
    expo = jnp.exp(attention_scores - new_top[..., None])
    total = jnp.sum(expo, axis=-1)
    attention_weights = expo.astype(jnp.bfloat16)
    reduced_sum = jnp.einsum(
        "shin,snhe->sihe", attention_weights, value_heads, preferred_element_type=jnp.float32
    )
    top, total, reduced_sum = (new_top, total, reduced_sum)
    attn = (
        (reduced_sum / total.transpose(0, 2, 1)[..., None])
        .reshape(samples, img_rows, resident_columns)
        .astype(jnp.bfloat16)
    )
    proj = jnp.einsum(
        "sin,nd->sid",
        attn,
        lax.all_gather(frozen_output_weight, "batch", axis=0, tiled=True),
        preferred_element_type=jnp.float32,
    )
    summed_heads = lax.psum(proj.astype(jnp.bfloat16), "mp").astype(jnp.float32)
    return (wide + gate * summed_heads).astype(jnp.bfloat16)


def flip(block, axis):
    return lax.ppermute(block, axis, [(0, 1), (1, 0)])


def swap_pair(block, split_axis, concat_axis):
    me = lax.axis_index("batch")
    half = block.shape[split_axis] // 2
    mine = lax.dynamic_slice_in_dim(block, me * half, half, split_axis)
    away = lax.dynamic_slice_in_dim(block, (1 - me) * half, half, split_axis)
    came = flip(away, "batch")
    first = jnp.where(me == 0, mine, came)
    second = jnp.where(me == 0, came, mine)
    return jnp.concatenate([first, second], axis=concat_axis)


def body_by_sample(
    image_token_states,
    timestep,
    prompt_token_length,
    modulation,
    text_key_value,
    frozen_query_key_value,
    frozen_output_weight,
    adapter_down_factors,
    adapter_up_factors,
    owner,
):
    samples, img_rows, width = image_token_states.shape
    txt_rows = text_key_value.shape[2]
    columns = frozen_query_key_value.shape[2]
    heads_here = columns // HEAD_SIZE
    steps_all = modulation.shape[0]
    at_seq = lax.axis_index("seq")
    at_mp = lax.axis_index("mp")
    at_core = lax.axis_index("batch")
    n_seq = 2 * samples

    up_mine = jnp.zeros(adapter_up_factors.shape[1:2] + adapter_up_factors.shape[3:], jnp.bfloat16)
    for which in range(3):
        up_mine = jnp.where(owner[which] == at_seq, adapter_up_factors[0][:, which], up_mine)
    up_mine = lax.dynamic_slice_in_dim(up_mine, at_core * columns, columns, 1)
    packed = jnp.concatenate([adapter_down_factors[0], up_mine], axis=1)
    packed = lax.all_gather(packed, "seq", axis=0)

    length_row = jnp.broadcast_to(
        prompt_token_length.astype(jnp.bfloat16)[:, None, None, None],
        (samples, 2, 1, text_key_value.shape[3]),
    )
    text = swap_pair(jnp.concatenate([text_key_value, length_row], axis=2), 3, 0)

    away_weight = flip(frozen_output_weight, "mp")
    weight_here = lax.all_gather(frozen_output_weight, "batch", axis=0, tiled=True)
    weight_away = lax.all_gather(away_weight, "batch", axis=0, tiled=True)

    onehot = (timestep[:, None] == jnp.arange(steps_all, dtype=jnp.int32)[None, :]).astype(
        jnp.float32
    )
    mods = jnp.einsum("st,tcd->scd", onehot, modulation, precision=lax.Precision.HIGHEST)
    shift = mods[:, 0][:, None, :]
    scale = mods[:, 1][:, None, :]
    gate = mods[:, 2][:, None, :]
    wide = image_token_states.astype(jnp.float32)

    rows_mp = img_rows // 2
    part = lax.dynamic_slice_in_dim(image_token_states, at_mp * rows_mp, rows_mp, 1).astype(
        jnp.float32
    )
    mean = jnp.mean(part, axis=-1, keepdims=True)
    centred = part - mean
    var = jnp.mean(centred * centred, axis=-1, keepdims=True)
    normed = (centred * lax.rsqrt(var + 1e-06) * (1.0 + scale) + shift).astype(jnp.bfloat16)

    piece = swap_pair(normed, 1, 0)
    piece = lax.all_to_all(piece, "seq", 0, 0, tiled=True)
    text = lax.all_to_all(text, "seq", 0, 0, tiled=True)
    piece_rows = piece.shape[1]
    whole = lax.all_gather(
        piece.reshape(n_seq * piece_rows, width), ("mp", "batch"), axis=0, tiled=True
    )

    triple = []
    for which in range(3):
        chosen = lax.dynamic_index_in_dim(packed, owner[which], 0, keepdims=False)
        delta = jnp.einsum(
            "rd,rn->dn", chosen[:, :width], chosen[:, width:], preferred_element_type=jnp.float32
        )
        merged = (frozen_query_key_value[:, which].astype(jnp.float32) + delta).astype(jnp.bfloat16)
        triple.append(
            jnp.dot(whole, merged, preferred_element_type=jnp.float32).astype(jnp.bfloat16)
        )
    queries, keys, values = triple
    tokens = queries.shape[0]
    text_keys = text[:, 0, :txt_rows].reshape(n_seq * txt_rows, columns)
    text_values = text[:, 1, :txt_rows].reshape(n_seq * txt_rows, columns)
    length = text[0, 0, txt_rows, 0].astype(jnp.int32)
    keys = jnp.concatenate([keys, text_keys], axis=0)
    values = jnp.concatenate([values, text_values], axis=0)
    position = jnp.arange(keys.shape[0], dtype=jnp.int32)
    live = position < tokens + length
    scores = (
        jnp.einsum(
            "ihe,nhe->hin",
            queries.reshape(-1, heads_here, HEAD_SIZE),
            keys.reshape(-1, heads_here, HEAD_SIZE),
            preferred_element_type=jnp.float32,
        )
        * HEAD_SIZE ** (-0.5)
    )
    scores = jnp.where(live[None, None, :], scores, -1e30)
    top = jnp.max(scores, axis=-1, keepdims=True)
    expo = jnp.exp(scores - top)
    total = jnp.sum(expo, axis=-1)
    summed = jnp.einsum(
        "hin,nhe->ihe",
        expo.astype(jnp.bfloat16),
        values.reshape(-1, heads_here, HEAD_SIZE),
        preferred_element_type=jnp.float32,
    )
    attn = (summed / total.T[:, :, None]).reshape(tokens, columns).astype(jnp.bfloat16)

    attn = attn.reshape(-1, n_seq, piece_rows, columns).transpose(1, 0, 2, 3)
    attn = lax.all_to_all(attn.reshape(n_seq, img_rows, columns), "seq", 0, 0, tiled=True)
    attn = swap_pair(attn, 0, 2)
    attn_away = flip(attn, "mp")
    proj = jnp.einsum("sin,nd->sid", attn, weight_here, preferred_element_type=jnp.float32)
    proj = proj + jnp.einsum(
        "sin,nd->sid", attn_away, weight_away, preferred_element_type=jnp.float32
    )
    return (wide + gate * proj).astype(jnp.bfloat16)


def pick(mesh):
    def run(*arrays):
        image, text = arrays[0], arrays[4]
        sizes = mesh.shape
        by_sample = (
            sizes["batch"] == 2
            and sizes["mp"] == 2
            and sizes["seq"] == 2 * image.shape[0]
            and image.shape[1] % 4 == 0
            and sizes["seq"] * text.shape[2] <= 256
        )
        return (body_by_sample if by_sample else body)(*arrays)

    return run


def solution(mesh):
    placed = (
        P(("groups", "batch"), "seq", None),
        P(("groups", "batch")),
        P(("groups", "batch")),
        P(),
        P(("groups", "batch"), None, "seq", "mp"),
        P(None, None, ("mp", "batch")),
        P(("mp", "batch"), None),
        P("seq", None, None),
        P("seq", None, None, "mp"),
        P(),
    )
    return jax.shard_map(
        pick(mesh),
        mesh=mesh,
        in_specs=placed,
        out_specs=P(("groups", "batch"), "seq", None),
        check_vma=False,
    )
```

```python
import jax
import jax.numpy as jnp
from jax import lax
from jax.sharding import PartitionSpec as P

HEAD_SIZE = 64


def broadcast(block, axis, source):
    block = jnp.where(lax.axis_index(axis) == source, block, jnp.zeros_like(block))
    return lax.psum(block, axis)


def body(
    image_token_states,
    timestep,
    prompt_token_length,
    modulation,
    text_key_value,
    frozen_query_key_value,
    frozen_output_weight,
    adapter_down_factors,
    adapter_up_factors,
    owner,
):
    samples, img_rows, width = image_token_states.shape
    txt_rows = text_key_value.shape[2]
    resident_columns = adapter_up_factors.shape[3]
    heads_here = resident_columns // HEAD_SIZE
    steps_all = modulation.shape[0]
    onehot = (timestep[:, None] == jnp.arange(steps_all, dtype=jnp.int32)[None, :]).astype(
        jnp.float32
    )
    mods = jnp.einsum("st,tcd->scd", onehot, modulation, precision=lax.Precision.HIGHEST)
    shift = mods[:, 0][:, None, :]
    scale = mods[:, 1][:, None, :]
    gate = mods[:, 2][:, None, :]
    wide = image_token_states.astype(jnp.float32)
    mean = jnp.mean(wide, axis=-1, keepdims=True)
    centred = wide - mean
    var = jnp.mean(centred * centred, axis=-1, keepdims=True)
    normed = (centred * lax.rsqrt(var + 1e-06) * (1.0 + scale) + shift).astype(jnp.bfloat16)
    down_list = []
    up_list = []
    for which in range(3):
        packed_tensor = jnp.concatenate(
            [adapter_down_factors[0], adapter_up_factors[0][:, which]], axis=1
        )
        packed_tensor = broadcast(packed_tensor, "seq", owner[which])
        down_list.append(packed_tensor[:, :width])
        up_list.append(packed_tensor[:, width:])
    down_factor = jnp.stack(down_list, axis=0)
    up_factor = jnp.stack(up_list, axis=1)
    delta = jnp.einsum("crd,rcn->dcn", down_factor, up_factor, preferred_element_type=jnp.float32)
    merged = (
        lax.all_gather(frozen_query_key_value, "batch", axis=2, tiled=True).astype(jnp.float32)
        + delta
    ).astype(jnp.bfloat16)
    qkv = jnp.einsum("sid,dcn->sicn", normed, merged, preferred_element_type=jnp.float32).astype(
        jnp.bfloat16
    )
    queries = qkv[:, :, 0]
    keys = jnp.concatenate([qkv[:, :, 1], text_key_value[:, 0]], axis=1)
    values = jnp.concatenate([qkv[:, :, 2], text_key_value[:, 1]], axis=1)
    query_heads = queries.reshape(samples, img_rows, heads_here, HEAD_SIZE)
    block = img_rows + txt_rows
    start_top = jnp.full((samples, heads_here, img_rows), -1e30, jnp.float32)
    top = start_top
    key_piece = lax.all_gather(keys, "seq", axis=1, tiled=True)
    value_piece = lax.all_gather(values, "seq", axis=1, tiled=True)
    count = key_piece.shape[1]
    position = jnp.arange(count, dtype=jnp.int32)
    shard = position // block
    inside = position % block
    text_index = shard * txt_rows + inside - img_rows
    live = (inside < img_rows)[None, :] | (text_index[None, :] < prompt_token_length[:, None])
    key_heads = key_piece.reshape(samples, count, heads_here, HEAD_SIZE)
    value_heads = value_piece.reshape(samples, count, heads_here, HEAD_SIZE)
    attention_scores = jnp.einsum(
        "sihe,snhe->shin", query_heads, key_heads, preferred_element_type=jnp.float32
    ) * HEAD_SIZE ** (-0.5)
    attention_scores = jnp.where(live[:, None, None, :], attention_scores, -1e30)
    new_top = jnp.maximum(top, jnp.max(attention_scores, axis=-1))
    expo = jnp.exp(attention_scores - new_top[..., None])
    total = jnp.sum(expo, axis=-1)
    attention_weights = expo.astype(jnp.bfloat16)
    reduced_sum = jnp.einsum(
        "shin,snhe->sihe", attention_weights, value_heads, preferred_element_type=jnp.float32
    )
    top, total, reduced_sum = (new_top, total, reduced_sum)
    attn = (
        (reduced_sum / total.transpose(0, 2, 1)[..., None])
        .reshape(samples, img_rows, resident_columns)
        .astype(jnp.bfloat16)
    )
    proj = jnp.einsum(
        "sin,nd->sid",
        attn,
        lax.all_gather(frozen_output_weight, "batch", axis=0, tiled=True),
        preferred_element_type=jnp.float32,
    )
    summed_heads = lax.psum(proj.astype(jnp.bfloat16), "mp").astype(jnp.float32)
    return (wide + gate * summed_heads).astype(jnp.bfloat16)


def flip(block, axis):
    return lax.ppermute(block, axis, [(0, 1), (1, 0)])


def swap_pair(block, split_axis, concat_axis):
    me = lax.axis_index("batch")
    half = block.shape[split_axis] // 2
    mine = lax.dynamic_slice_in_dim(block, me * half, half, split_axis)
    away = lax.dynamic_slice_in_dim(block, (1 - me) * half, half, split_axis)
    came = flip(away, "batch")
    first = jnp.where(me == 0, mine, came)
    second = jnp.where(me == 0, came, mine)
    return jnp.concatenate([first, second], axis=concat_axis)


def body_by_sample(
    image_token_states,
    timestep,
    prompt_token_length,
    modulation,
    text_key_value,
    frozen_query_key_value,
    frozen_output_weight,
    adapter_down_factors,
    adapter_up_factors,
    owner,
):
    samples, img_rows, width = image_token_states.shape
    txt_rows = text_key_value.shape[2]
    columns = frozen_query_key_value.shape[2]
    heads_here = columns // HEAD_SIZE
    steps_all = modulation.shape[0]
    at_seq = lax.axis_index("seq")
    at_mp = lax.axis_index("mp")
    at_core = lax.axis_index("batch")
    n_seq = 2 * samples

    up_mine = jnp.zeros(adapter_up_factors.shape[1:2] + adapter_up_factors.shape[3:], jnp.bfloat16)
    for which in range(3):
        up_mine = jnp.where(owner[which] == at_seq, adapter_up_factors[0][:, which], up_mine)
    up_mine = lax.dynamic_slice_in_dim(up_mine, at_core * columns, columns, 1)
    packed = jnp.concatenate([adapter_down_factors[0], up_mine], axis=1)
    packed = lax.all_gather(packed, "seq", axis=0)

    length_row = jnp.broadcast_to(
        prompt_token_length.astype(jnp.bfloat16)[:, None, None, None],
        (samples, 2, 1, text_key_value.shape[3]),
    )
    text = swap_pair(jnp.concatenate([text_key_value, length_row], axis=2), 3, 0)
    text = lax.all_gather(text, "seq", axis=0)
    text = lax.dynamic_index_in_dim(text, at_seq, 1, keepdims=False)

    away_weight = flip(frozen_output_weight, "mp")

    onehot = (timestep[:, None] == jnp.arange(steps_all, dtype=jnp.int32)[None, :]).astype(
        jnp.float32
    )
    mods = jnp.einsum("st,tcd->scd", onehot, modulation, precision=lax.Precision.HIGHEST)
    shift = mods[:, 0][:, None, :]
    scale = mods[:, 1][:, None, :]
    gate = mods[:, 2][:, None, :]
    wide = image_token_states.astype(jnp.float32)

    rows_mp = img_rows // 2
    part = lax.dynamic_slice_in_dim(image_token_states, at_mp * rows_mp, rows_mp, 1).astype(
        jnp.float32
    )
    mean = jnp.mean(part, axis=-1, keepdims=True)
    centred = part - mean
    var = jnp.mean(centred * centred, axis=-1, keepdims=True)
    normed = (centred * lax.rsqrt(var + 1e-06) * (1.0 + scale) + shift).astype(jnp.bfloat16)

    piece = swap_pair(normed, 1, 0)
    piece = lax.all_to_all(piece, "seq", 0, 0, tiled=True)
    piece_rows = piece.shape[1]
    piece = piece.reshape(n_seq * piece_rows, width)
    piece_mp = flip(piece, "mp")
    piece_core = flip(piece, "batch")
    piece_both = flip(piece_mp, "batch")
    merged = []
    for which in range(3):
        chosen = lax.dynamic_index_in_dim(packed, owner[which], 0, keepdims=False)
        delta = jnp.einsum(
            "rd,rn->dn", chosen[:, :width], chosen[:, width:], preferred_element_type=jnp.float32
        )
        merged.append(
            (frozen_query_key_value[:, which].astype(jnp.float32) + delta).astype(jnp.bfloat16)
        )
    merged = lax.optimization_barrier(merged)
    early = jnp.concatenate([piece, piece_core], axis=0)
    late = jnp.concatenate([piece_mp, piece_both], axis=0)
    triple = []
    halves = [
        [jnp.dot(rows, m, preferred_element_type=jnp.float32).astype(jnp.bfloat16) for m in merged]
        for rows in (early, late)
    ]
    for which in range(3):
        triple.append(jnp.concatenate([halves[0][which], halves[1][which]], axis=0))
    queries, keys, values = triple
    away_weight, queries = lax.optimization_barrier((away_weight, queries))
    weight_here = lax.all_gather(frozen_output_weight, "batch", axis=0, tiled=True)
    weight_away = lax.all_gather(away_weight, "batch", axis=0, tiled=True)
    tokens = queries.shape[0]
    text_keys = text[:, 0, :txt_rows].reshape(n_seq * txt_rows, columns)
    text_values = text[:, 1, :txt_rows].reshape(n_seq * txt_rows, columns)
    length = text[0, 0, txt_rows, 0].astype(jnp.int32)
    keys = jnp.concatenate([keys, text_keys], axis=0)
    values = jnp.concatenate([values, text_values], axis=0)
    position = jnp.arange(keys.shape[0], dtype=jnp.int32)
    live = position < tokens + length
    scores = (
        jnp.einsum(
            "ihe,nhe->hin",
            queries.reshape(-1, heads_here, HEAD_SIZE),
            keys.reshape(-1, heads_here, HEAD_SIZE),
            preferred_element_type=jnp.float32,
        )
        * HEAD_SIZE ** (-0.5)
    )
    scores = jnp.where(live[None, None, :], scores, -1e30)
    top = jnp.max(scores, axis=-1, keepdims=True)
    expo = jnp.exp(scores - top)
    total = jnp.sum(expo, axis=-1)
    summed = jnp.einsum(
        "hin,nhe->ihe",
        expo.astype(jnp.bfloat16),
        values.reshape(-1, heads_here, HEAD_SIZE),
        preferred_element_type=jnp.float32,
    )
    attn = (summed / total.T[:, :, None]).reshape(tokens, columns).astype(jnp.bfloat16)

    attn = attn.reshape(2, 2, n_seq, piece_rows, columns)
    attn = jnp.where(at_mp == 0, attn, attn[::-1])
    attn = jnp.where(at_core == 0, attn, attn[:, ::-1])
    attn = attn.reshape(4, n_seq, piece_rows, columns).transpose(1, 0, 2, 3)
    attn = lax.all_to_all(attn.reshape(n_seq, img_rows, columns), "seq", 0, 0, tiled=True)
    attn = swap_pair(attn, 0, 2)
    attn_away = flip(attn, "mp")
    proj = jnp.einsum("sin,nd->sid", attn, weight_here, preferred_element_type=jnp.float32)
    proj = proj + jnp.einsum(
        "sin,nd->sid", attn_away, weight_away, preferred_element_type=jnp.float32
    )
    return (wide + gate * proj).astype(jnp.bfloat16)


def pick(mesh):
    def run(*arrays):
        image, text = arrays[0], arrays[4]
        sizes = mesh.shape
        by_sample = (
            sizes["batch"] == 2
            and sizes["mp"] == 2
            and sizes["seq"] == 2 * image.shape[0]
            and image.shape[1] % 4 == 0
            and sizes["seq"] * text.shape[2] <= 256
        )
        return (body_by_sample if by_sample else body)(*arrays)

    return run


def solution(mesh):
    placed = (
        P(("groups", "batch"), "seq", None),
        P(("groups", "batch")),
        P(("groups", "batch")),
        P(),
        P(("groups", "batch"), None, "seq", "mp"),
        P(None, None, ("mp", "batch")),
        P(("mp", "batch"), None),
        P("seq", None, None),
        P("seq", None, None, "mp"),
        P(),
    )
    return jax.shard_map(
        pick(mesh),
        mesh=mesh,
        in_specs=placed,
        out_specs=P(("groups", "batch"), "seq", None),
        check_vma=False,
    )
```

```python
import jax
import jax.numpy as jnp
from jax import lax
from jax.sharding import PartitionSpec as P

HEAD_SIZE = 64


def broadcast(block, axis, source):
    block = jnp.where(lax.axis_index(axis) == source, block, jnp.zeros_like(block))
    return lax.psum(block, axis)


def body(
    image_token_states,
    timestep,
    prompt_token_length,
    modulation,
    text_key_value,
    frozen_query_key_value,
    frozen_output_weight,
    adapter_down_factors,
    adapter_up_factors,
    owner,
):
    samples, img_rows, width = image_token_states.shape
    txt_rows = text_key_value.shape[2]
    resident_columns = adapter_up_factors.shape[3]
    heads_here = resident_columns // HEAD_SIZE
    steps_all = modulation.shape[0]
    onehot = (timestep[:, None] == jnp.arange(steps_all, dtype=jnp.int32)[None, :]).astype(
        jnp.float32
    )
    mods = jnp.einsum("st,tcd->scd", onehot, modulation, precision=lax.Precision.HIGHEST)
    shift = mods[:, 0][:, None, :]
    scale = mods[:, 1][:, None, :]
    gate = mods[:, 2][:, None, :]
    wide = image_token_states.astype(jnp.float32)
    mean = jnp.mean(wide, axis=-1, keepdims=True)
    centred = wide - mean
    var = jnp.mean(centred * centred, axis=-1, keepdims=True)
    normed = (centred * lax.rsqrt(var + 1e-06) * (1.0 + scale) + shift).astype(jnp.bfloat16)
    down_list = []
    up_list = []
    for which in range(3):
        packed_tensor = jnp.concatenate(
            [adapter_down_factors[0], adapter_up_factors[0][:, which]], axis=1
        )
        packed_tensor = broadcast(packed_tensor, "seq", owner[which])
        down_list.append(packed_tensor[:, :width])
        up_list.append(packed_tensor[:, width:])
    down_factor = jnp.stack(down_list, axis=0)
    up_factor = jnp.stack(up_list, axis=1)
    delta = jnp.einsum("crd,rcn->dcn", down_factor, up_factor, preferred_element_type=jnp.float32)
    merged = (
        lax.all_gather(frozen_query_key_value, "batch", axis=2, tiled=True).astype(jnp.float32)
        + delta
    ).astype(jnp.bfloat16)
    qkv = jnp.einsum("sid,dcn->sicn", normed, merged, preferred_element_type=jnp.float32).astype(
        jnp.bfloat16
    )
    queries = qkv[:, :, 0]
    keys = jnp.concatenate([qkv[:, :, 1], text_key_value[:, 0]], axis=1)
    values = jnp.concatenate([qkv[:, :, 2], text_key_value[:, 1]], axis=1)
    query_heads = queries.reshape(samples, img_rows, heads_here, HEAD_SIZE)
    block = img_rows + txt_rows
    start_top = jnp.full((samples, heads_here, img_rows), -1e30, jnp.float32)
    top = start_top
    key_piece = lax.all_gather(keys, "seq", axis=1, tiled=True)
    value_piece = lax.all_gather(values, "seq", axis=1, tiled=True)
    count = key_piece.shape[1]
    position = jnp.arange(count, dtype=jnp.int32)
    shard = position // block
    inside = position % block
    text_index = shard * txt_rows + inside - img_rows
    live = (inside < img_rows)[None, :] | (text_index[None, :] < prompt_token_length[:, None])
    key_heads = key_piece.reshape(samples, count, heads_here, HEAD_SIZE)
    value_heads = value_piece.reshape(samples, count, heads_here, HEAD_SIZE)
    attention_scores = jnp.einsum(
        "sihe,snhe->shin", query_heads, key_heads, preferred_element_type=jnp.float32
    ) * HEAD_SIZE ** (-0.5)
    attention_scores = jnp.where(live[:, None, None, :], attention_scores, -1e30)
    new_top = jnp.maximum(top, jnp.max(attention_scores, axis=-1))
    expo = jnp.exp(attention_scores - new_top[..., None])
    total = jnp.sum(expo, axis=-1)
    attention_weights = expo.astype(jnp.bfloat16)
    reduced_sum = jnp.einsum(
        "shin,snhe->sihe", attention_weights, value_heads, preferred_element_type=jnp.float32
    )
    top, total, reduced_sum = (new_top, total, reduced_sum)
    attn = (
        (reduced_sum / total.transpose(0, 2, 1)[..., None])
        .reshape(samples, img_rows, resident_columns)
        .astype(jnp.bfloat16)
    )
    proj = jnp.einsum(
        "sin,nd->sid",
        attn,
        lax.all_gather(frozen_output_weight, "batch", axis=0, tiled=True),
        preferred_element_type=jnp.float32,
    )
    summed_heads = lax.psum(proj.astype(jnp.bfloat16), "mp").astype(jnp.float32)
    return (wide + gate * summed_heads).astype(jnp.bfloat16)


def flip(block, axis):
    return lax.ppermute(block, axis, [(0, 1), (1, 0)])


def swap_pair(block, split_axis, concat_axis):
    me = lax.axis_index("batch")
    half = block.shape[split_axis] // 2
    mine = lax.dynamic_slice_in_dim(block, me * half, half, split_axis)
    away = lax.dynamic_slice_in_dim(block, (1 - me) * half, half, split_axis)
    came = flip(away, "batch")
    first = jnp.where(me == 0, mine, came)
    second = jnp.where(me == 0, came, mine)
    return jnp.concatenate([first, second], axis=concat_axis)


def body_by_sample(
    image_token_states,
    timestep,
    prompt_token_length,
    modulation,
    text_key_value,
    frozen_query_key_value,
    frozen_output_weight,
    adapter_down_factors,
    adapter_up_factors,
    owner,
):
    samples, img_rows, width = image_token_states.shape
    txt_rows = text_key_value.shape[2]
    columns = frozen_query_key_value.shape[2]
    heads_here = columns // HEAD_SIZE
    steps_all = modulation.shape[0]
    at_seq = lax.axis_index("seq")
    at_mp = lax.axis_index("mp")
    at_core = lax.axis_index("batch")
    n_seq = 2 * samples

    up_mine = jnp.zeros(adapter_up_factors.shape[1:2] + adapter_up_factors.shape[3:], jnp.bfloat16)
    for which in range(3):
        up_mine = jnp.where(owner[which] == at_seq, adapter_up_factors[0][:, which], up_mine)
    up_mine = lax.dynamic_slice_in_dim(up_mine, at_core * columns, columns, 1)
    half_rank = up_mine.shape[0] // 2
    down_mine = lax.dynamic_slice_in_dim(adapter_down_factors[0], at_core * half_rank, half_rank, 0)
    packed = jnp.concatenate([down_mine, up_mine[:half_rank], up_mine[half_rank:]], axis=1)
    packed = lax.all_gather(packed, "seq", axis=0)

    length_row = jnp.broadcast_to(
        prompt_token_length.astype(jnp.bfloat16)[:, None, None, None],
        (samples, 2, 1, text_key_value.shape[3]),
    )
    text = swap_pair(jnp.concatenate([text_key_value, length_row], axis=2), 3, 0)
    text_shape = text.shape
    text = text.reshape(n_seq, -1)
    text_size = text.shape[1]

    away_weight = flip(frozen_output_weight, "mp")

    onehot = (timestep[:, None] == jnp.arange(steps_all, dtype=jnp.int32)[None, :]).astype(
        jnp.float32
    )
    mods = jnp.einsum("st,tcd->scd", onehot, modulation, precision=lax.Precision.HIGHEST)
    shift = mods[:, 0][:, None, :]
    scale = mods[:, 1][:, None, :]
    gate = mods[:, 2][:, None, :]
    wide = image_token_states.astype(jnp.float32)

    rows_mp = img_rows // 2
    part = lax.dynamic_slice_in_dim(image_token_states, at_mp * rows_mp, rows_mp, 1).astype(
        jnp.float32
    )
    mean = jnp.mean(part, axis=-1, keepdims=True)
    centred = part - mean
    var = jnp.mean(centred * centred, axis=-1, keepdims=True)
    normed = (centred * lax.rsqrt(var + 1e-06) * (1.0 + scale) + shift).astype(jnp.bfloat16)

    piece = swap_pair(normed, 1, 0)
    piece_rows = piece.shape[1]
    extra = -(-text_size // width)
    text = jnp.pad(text, ((0, 0), (0, extra * width - text_size))).reshape(n_seq, extra, width)
    piece = jnp.concatenate([piece, text], axis=1)
    piece = lax.all_to_all(piece, "seq", 0, 0, tiled=True)
    text = piece[:, piece_rows:].reshape(n_seq, extra * width)[:, :text_size].reshape(text_shape)
    piece = piece[:, :piece_rows]
    piece = piece.reshape(n_seq * piece_rows, width)
    piece_mp = flip(piece, "mp")
    piece_core = flip(piece, "batch")
    piece_both = flip(piece_mp, "batch")
    merged = []
    chosen = jnp.stack(
        [lax.dynamic_index_in_dim(packed, owner[which], 0, keepdims=False) for which in range(3)]
    )
    down_mine = chosen[:, :, :width]
    down_came = flip(down_mine, "batch")
    down_all = jnp.concatenate(
        [
            jnp.where(at_core == 0, down_mine, down_came),
            jnp.where(at_core == 0, down_came, down_mine),
        ],
        axis=1,
    )
    up_all = jnp.concatenate(
        [chosen[:, :, width : width + columns], chosen[:, :, width + columns :]], axis=1
    )
    for which in range(3):
        delta = jnp.einsum(
            "rd,rn->dn", down_all[which], up_all[which], preferred_element_type=jnp.float32
        )
        merged.append(
            (frozen_query_key_value[:, which].astype(jnp.float32) + delta).astype(jnp.bfloat16)
        )
    merged = lax.optimization_barrier(merged)
    early = jnp.concatenate([piece, piece_core], axis=0)
    late = jnp.concatenate([piece_mp, piece_both], axis=0)
    triple = []
    halves = [
        [jnp.dot(rows, m, preferred_element_type=jnp.float32).astype(jnp.bfloat16) for m in merged]
        for rows in (early, late)
    ]
    for which in range(3):
        triple.append(jnp.concatenate([halves[0][which], halves[1][which]], axis=0))
    queries, keys, values = triple
    away_weight, queries = lax.optimization_barrier((away_weight, queries))
    weight_here = lax.all_gather(frozen_output_weight, "batch", axis=0, tiled=True)
    weight_away = lax.all_gather(away_weight, "batch", axis=0, tiled=True)
    tokens = queries.shape[0]
    text_keys = text[:, 0, :txt_rows].reshape(n_seq * txt_rows, columns)
    text_values = text[:, 1, :txt_rows].reshape(n_seq * txt_rows, columns)
    length = text[0, 0, txt_rows, 0].astype(jnp.int32)
    keys = jnp.concatenate([keys, text_keys], axis=0)
    values = jnp.concatenate([values, text_values], axis=0)
    position = jnp.arange(keys.shape[0], dtype=jnp.int32)
    live = position < tokens + length
    scores = (
        jnp.einsum(
            "ihe,nhe->hin",
            queries.reshape(-1, heads_here, HEAD_SIZE),
            keys.reshape(-1, heads_here, HEAD_SIZE),
            preferred_element_type=jnp.float32,
        )
        * HEAD_SIZE ** (-0.5)
    )
    scores = jnp.where(live[None, None, :], scores, -1e30)
    top = jnp.max(scores, axis=-1, keepdims=True)
    expo = jnp.exp(scores - top)
    total = jnp.sum(expo, axis=-1)
    summed = jnp.einsum(
        "hin,nhe->ihe",
        expo.astype(jnp.bfloat16),
        values.reshape(-1, heads_here, HEAD_SIZE),
        preferred_element_type=jnp.float32,
    )
    attn = (summed / total.T[:, :, None]).reshape(tokens, columns).astype(jnp.bfloat16)

    attn = attn.reshape(2, 2, n_seq, piece_rows, columns)
    attn = jnp.where(at_mp == 0, attn, attn[::-1])
    attn = jnp.where(at_core == 0, attn, attn[:, ::-1])
    attn = attn.reshape(4, n_seq, piece_rows, columns).transpose(1, 0, 2, 3)
    attn = lax.all_to_all(attn.reshape(n_seq, img_rows, columns), "seq", 0, 0, tiled=True)
    attn = swap_pair(attn, 0, 2)
    attn_away = flip(attn, "mp")
    proj = jnp.einsum("sin,nd->sid", attn, weight_here, preferred_element_type=jnp.float32)
    proj = lax.optimization_barrier(proj)
    proj = proj + jnp.einsum(
        "sin,nd->sid", attn_away, weight_away, preferred_element_type=jnp.float32
    )
    return (wide + gate * proj).astype(jnp.bfloat16)


def pick(mesh):
    def run(*arrays):
        image, text = arrays[0], arrays[4]
        sizes = mesh.shape
        by_sample = (
            sizes["batch"] == 2
            and sizes["mp"] == 2
            and sizes["seq"] == 2 * image.shape[0]
            and image.shape[1] % 4 == 0
            and arrays[7].shape[1] % 2 == 0
            and sizes["seq"] * text.shape[2] <= 256
        )
        return (body_by_sample if by_sample else body)(*arrays)

    return run


def solution(mesh):
    placed = (
        P(("groups", "batch"), "seq", None),
        P(("groups", "batch")),
        P(("groups", "batch")),
        P(),
        P(("groups", "batch"), None, "seq", "mp"),
        P(None, None, ("mp", "batch")),
        P(("mp", "batch"), None),
        P("seq", None, None),
        P("seq", None, None, "mp"),
        P(),
    )
    return jax.shard_map(
        pick(mesh),
        mesh=mesh,
        in_specs=placed,
        out_specs=P(("groups", "batch"), "seq", None),
        check_vma=False,
    )
```

```python
import jax
import jax.numpy as jnp
from jax import lax
from jax.sharding import PartitionSpec as P

HEAD_SIZE = 64


def broadcast(block, axis, source):
    block = jnp.where(lax.axis_index(axis) == source, block, jnp.zeros_like(block))
    return lax.psum(block, axis)


def body(
    image_token_states,
    timestep,
    prompt_token_length,
    modulation,
    text_key_value,
    frozen_query_key_value,
    frozen_output_weight,
    adapter_down_factors,
    adapter_up_factors,
    owner,
):
    samples, img_rows, width = image_token_states.shape
    txt_rows = text_key_value.shape[2]
    resident_columns = adapter_up_factors.shape[3]
    heads_here = resident_columns // HEAD_SIZE
    steps_all = modulation.shape[0]
    onehot = (timestep[:, None] == jnp.arange(steps_all, dtype=jnp.int32)[None, :]).astype(
        jnp.float32
    )
    mods = jnp.einsum("st,tcd->scd", onehot, modulation, precision=lax.Precision.HIGHEST)
    shift = mods[:, 0][:, None, :]
    scale = mods[:, 1][:, None, :]
    gate = mods[:, 2][:, None, :]
    wide = image_token_states.astype(jnp.float32)
    mean = jnp.mean(wide, axis=-1, keepdims=True)
    centred = wide - mean
    var = jnp.mean(centred * centred, axis=-1, keepdims=True)
    normed = (centred * lax.rsqrt(var + 1e-06) * (1.0 + scale) + shift).astype(jnp.bfloat16)
    down_list = []
    up_list = []
    for which in range(3):
        packed_tensor = jnp.concatenate(
            [adapter_down_factors[0], adapter_up_factors[0][:, which]], axis=1
        )
        packed_tensor = broadcast(packed_tensor, "seq", owner[which])
        down_list.append(packed_tensor[:, :width])
        up_list.append(packed_tensor[:, width:])
    down_factor = jnp.stack(down_list, axis=0)
    up_factor = jnp.stack(up_list, axis=1)
    delta = jnp.einsum("crd,rcn->dcn", down_factor, up_factor, preferred_element_type=jnp.float32)
    merged = (
        lax.all_gather(frozen_query_key_value, "batch", axis=2, tiled=True).astype(jnp.float32)
        + delta
    ).astype(jnp.bfloat16)
    qkv = jnp.einsum("sid,dcn->sicn", normed, merged, preferred_element_type=jnp.float32).astype(
        jnp.bfloat16
    )
    queries = qkv[:, :, 0]
    keys = jnp.concatenate([qkv[:, :, 1], text_key_value[:, 0]], axis=1)
    values = jnp.concatenate([qkv[:, :, 2], text_key_value[:, 1]], axis=1)
    query_heads = queries.reshape(samples, img_rows, heads_here, HEAD_SIZE)
    block = img_rows + txt_rows
    start_top = jnp.full((samples, heads_here, img_rows), -1e30, jnp.float32)
    top = start_top
    key_piece = lax.all_gather(keys, "seq", axis=1, tiled=True)
    value_piece = lax.all_gather(values, "seq", axis=1, tiled=True)
    count = key_piece.shape[1]
    position = jnp.arange(count, dtype=jnp.int32)
    shard = position // block
    inside = position % block
    text_index = shard * txt_rows + inside - img_rows
    live = (inside < img_rows)[None, :] | (text_index[None, :] < prompt_token_length[:, None])
    key_heads = key_piece.reshape(samples, count, heads_here, HEAD_SIZE)
    value_heads = value_piece.reshape(samples, count, heads_here, HEAD_SIZE)
    attention_scores = jnp.einsum(
        "sihe,snhe->shin", query_heads, key_heads, preferred_element_type=jnp.float32
    ) * HEAD_SIZE ** (-0.5)
    attention_scores = jnp.where(live[:, None, None, :], attention_scores, -1e30)
    new_top = jnp.maximum(top, jnp.max(attention_scores, axis=-1))
    expo = jnp.exp(attention_scores - new_top[..., None])
    total = jnp.sum(expo, axis=-1)
    attention_weights = expo.astype(jnp.bfloat16)
    reduced_sum = jnp.einsum(
        "shin,snhe->sihe", attention_weights, value_heads, preferred_element_type=jnp.float32
    )
    top, total, reduced_sum = (new_top, total, reduced_sum)
    attn = (
        (reduced_sum / total.transpose(0, 2, 1)[..., None])
        .reshape(samples, img_rows, resident_columns)
        .astype(jnp.bfloat16)
    )
    proj = jnp.einsum(
        "sin,nd->sid",
        attn,
        lax.all_gather(frozen_output_weight, "batch", axis=0, tiled=True),
        preferred_element_type=jnp.float32,
    )
    summed_heads = lax.psum(proj.astype(jnp.bfloat16), "mp").astype(jnp.float32)
    return (wide + gate * summed_heads).astype(jnp.bfloat16)


def flip(block, axis):
    return lax.ppermute(block, axis, [(0, 1), (1, 0)])


def swap_pair(block, split_axis, concat_axis):
    me = lax.axis_index("batch")
    half = block.shape[split_axis] // 2
    mine = lax.dynamic_slice_in_dim(block, me * half, half, split_axis)
    away = lax.dynamic_slice_in_dim(block, (1 - me) * half, half, split_axis)
    came = flip(away, "batch")
    first = jnp.where(me == 0, mine, came)
    second = jnp.where(me == 0, came, mine)
    return jnp.concatenate([first, second], axis=concat_axis)


def body_by_sample(
    image_token_states,
    timestep,
    prompt_token_length,
    modulation,
    text_key_value,
    frozen_query_key_value,
    frozen_output_weight,
    adapter_down_factors,
    adapter_up_factors,
    owner,
):
    samples, img_rows, width = image_token_states.shape
    txt_rows = text_key_value.shape[2]
    columns = frozen_query_key_value.shape[2]
    heads_here = columns // HEAD_SIZE
    steps_all = modulation.shape[0]
    at_seq = lax.axis_index("seq")
    at_mp = lax.axis_index("mp")
    at_core = lax.axis_index("batch")
    n_seq = 2 * samples

    up_mine = jnp.zeros(adapter_up_factors.shape[1:2] + adapter_up_factors.shape[3:], jnp.bfloat16)
    for which in range(3):
        up_mine = jnp.where(owner[which] == at_seq, adapter_up_factors[0][:, which], up_mine)
    up_mine = lax.dynamic_slice_in_dim(up_mine, at_core * columns, columns, 1)
    half_rank = up_mine.shape[0] // 2
    down_mine = lax.dynamic_slice_in_dim(adapter_down_factors[0], at_core * half_rank, half_rank, 0)
    packed = jnp.concatenate([down_mine, up_mine[:half_rank], up_mine[half_rank:]], axis=1)
    packed = lax.all_gather(packed, "seq", axis=0)

    length_row = jnp.broadcast_to(
        prompt_token_length.astype(jnp.bfloat16)[:, None, None, None],
        (samples, 2, 1, text_key_value.shape[3]),
    )
    text = swap_pair(jnp.concatenate([text_key_value, length_row], axis=2), 3, 0)
    text_shape = text.shape
    text = text.reshape(n_seq, -1)
    text_size = text.shape[1]

    away_weight = flip(frozen_output_weight, "mp")

    onehot = (timestep[:, None] == jnp.arange(steps_all, dtype=jnp.int32)[None, :]).astype(
        jnp.float32
    )
    mods = jnp.einsum("st,tcd->scd", onehot, modulation, precision=lax.Precision.HIGHEST)
    shift = mods[:, 0][:, None, :]
    scale = mods[:, 1][:, None, :]
    gate = mods[:, 2][:, None, :]
    wide = image_token_states.astype(jnp.float32)

    rows_mp = img_rows // 2
    part = lax.dynamic_slice_in_dim(image_token_states, at_mp * rows_mp, rows_mp, 1).astype(
        jnp.float32
    )
    mean = jnp.mean(part, axis=-1, keepdims=True)
    centred = part - mean
    var = jnp.mean(centred * centred, axis=-1, keepdims=True)
    normed = (centred * lax.rsqrt(var + 1e-06) * (1.0 + scale) + shift).astype(jnp.bfloat16)

    piece = swap_pair(normed, 1, 0)
    piece_rows = piece.shape[1]
    extra = -(-text_size // width)
    text = jnp.pad(text, ((0, 0), (0, extra * width - text_size))).reshape(n_seq, extra, width)
    piece = jnp.concatenate([piece, text], axis=1)
    piece = lax.all_to_all(piece, "seq", 0, 0, tiled=True)
    text = piece[:, piece_rows:].reshape(n_seq, extra * width)[:, :text_size].reshape(text_shape)
    piece = piece[:, :piece_rows]
    piece = piece.reshape(n_seq * piece_rows, width)
    piece_mp = flip(piece, "mp")
    piece_core = flip(piece, "batch")
    piece_both = flip(piece_mp, "batch")
    merged = []
    chosen = jnp.stack(
        [lax.dynamic_index_in_dim(packed, owner[which], 0, keepdims=False) for which in range(3)]
    )
    down_mine = chosen[:, :, :width]
    down_came = flip(down_mine, "batch")
    down_all = jnp.concatenate(
        [
            jnp.where(at_core == 0, down_mine, down_came),
            jnp.where(at_core == 0, down_came, down_mine),
        ],
        axis=1,
    )
    up_all = jnp.concatenate(
        [chosen[:, :, width : width + columns], chosen[:, :, width + columns :]], axis=1
    )
    for which in range(3):
        delta = jnp.einsum(
            "rd,rn->dn", down_all[which], up_all[which], preferred_element_type=jnp.float32
        )
        merged.append(
            (frozen_query_key_value[:, which].astype(jnp.float32) + delta).astype(jnp.bfloat16)
        )
    merged = lax.optimization_barrier(merged)
    early = jnp.concatenate([piece, piece_core], axis=0)
    late = jnp.concatenate([piece_mp, piece_both], axis=0)
    triple = []
    halves = [
        [jnp.dot(rows, m, preferred_element_type=jnp.float32).astype(jnp.bfloat16) for m in merged]
        for rows in (early, late)
    ]
    halves[0] = lax.optimization_barrier(halves[0])
    for which in range(3):
        triple.append(jnp.concatenate([halves[0][which], halves[1][which]], axis=0))
    queries, keys, values = triple
    away_weight, queries = lax.optimization_barrier((away_weight, queries))
    weight_here = lax.all_gather(frozen_output_weight, "batch", axis=0, tiled=True)
    weight_away = lax.all_gather(away_weight, "batch", axis=0, tiled=True)
    tokens = queries.shape[0]
    text_keys = text[:, 0, :txt_rows].reshape(n_seq * txt_rows, columns)
    text_values = text[:, 1, :txt_rows].reshape(n_seq * txt_rows, columns)
    length = text[0, 0, txt_rows, 0].astype(jnp.int32)
    keys = jnp.concatenate([keys, text_keys], axis=0)
    values = jnp.concatenate([values, text_values], axis=0)
    position = jnp.arange(keys.shape[0], dtype=jnp.int32)
    live = position < tokens + length
    scores = (
        jnp.einsum(
            "ihe,nhe->hin",
            queries.reshape(-1, heads_here, HEAD_SIZE),
            keys.reshape(-1, heads_here, HEAD_SIZE),
            preferred_element_type=jnp.float32,
        )
        * HEAD_SIZE ** (-0.5)
    )
    scores = jnp.where(live[None, None, :], scores, -1e30)
    top = jnp.max(scores, axis=-1, keepdims=True)
    expo = jnp.exp(scores - top)
    total = jnp.sum(expo, axis=-1)
    summed = jnp.einsum(
        "hin,nhe->ihe",
        expo.astype(jnp.bfloat16),
        values.reshape(-1, heads_here, HEAD_SIZE),
        preferred_element_type=jnp.float32,
    )
    attn = (summed / total.T[:, :, None]).reshape(tokens, columns).astype(jnp.bfloat16)

    attn = attn.reshape(2, 2, n_seq, piece_rows, columns)
    attn = jnp.where(at_mp == 0, attn, attn[::-1])
    attn = jnp.where(at_core == 0, attn, attn[:, ::-1])
    attn = attn.reshape(4, n_seq, piece_rows, columns).transpose(1, 0, 2, 3)
    attn = lax.all_to_all(attn.reshape(n_seq, img_rows, columns), "seq", 0, 0, tiled=True)
    attn = swap_pair(attn, 0, 2)
    attn_away = flip(attn, "mp")
    proj = jnp.einsum("sin,nd->sid", attn, weight_here, preferred_element_type=jnp.float32)
    proj = lax.optimization_barrier(proj)
    proj = proj + jnp.einsum(
        "sin,nd->sid", attn_away, weight_away, preferred_element_type=jnp.float32
    )
    return (wide + gate * proj).astype(jnp.bfloat16)


def pick(mesh):
    def run(*arrays):
        image, text = arrays[0], arrays[4]
        sizes = mesh.shape
        by_sample = (
            sizes["batch"] == 2
            and sizes["mp"] == 2
            and sizes["seq"] == 2 * image.shape[0]
            and image.shape[1] % 4 == 0
            and arrays[7].shape[1] % 2 == 0
            and sizes["seq"] * text.shape[2] <= 256
        )
        return (body_by_sample if by_sample else body)(*arrays)

    return run


def solution(mesh):
    placed = (
        P(("groups", "batch"), "seq", None),
        P(("groups", "batch")),
        P(("groups", "batch")),
        P(),
        P(("groups", "batch"), None, "seq", "mp"),
        P(None, None, ("mp", "batch")),
        P(("mp", "batch"), None),
        P("seq", None, None),
        P("seq", None, None, "mp"),
        P(),
    )
    return jax.shard_map(
        pick(mesh),
        mesh=mesh,
        in_specs=placed,
        out_specs=P(("groups", "batch"), "seq", None),
        check_vma=False,
    )
```

```python
import jax
import jax.numpy as jnp
from jax import lax
from jax.sharding import PartitionSpec as P

HEAD_SIZE = 64


def broadcast(block, axis, source):
    block = jnp.where(lax.axis_index(axis) == source, block, jnp.zeros_like(block))
    return lax.psum(block, axis)


def body(
    image_token_states,
    timestep,
    prompt_token_length,
    modulation,
    text_key_value,
    frozen_query_key_value,
    frozen_output_weight,
    adapter_down_factors,
    adapter_up_factors,
    owner,
):
    samples, img_rows, width = image_token_states.shape
    txt_rows = text_key_value.shape[2]
    resident_columns = adapter_up_factors.shape[3]
    heads_here = resident_columns // HEAD_SIZE
    steps_all = modulation.shape[0]
    onehot = (timestep[:, None] == jnp.arange(steps_all, dtype=jnp.int32)[None, :]).astype(
        jnp.float32
    )
    mods = jnp.einsum("st,tcd->scd", onehot, modulation, precision=lax.Precision.HIGHEST)
    shift = mods[:, 0][:, None, :]
    scale = mods[:, 1][:, None, :]
    gate = mods[:, 2][:, None, :]
    wide = image_token_states.astype(jnp.float32)
    mean = jnp.mean(wide, axis=-1, keepdims=True)
    centred = wide - mean
    var = jnp.mean(centred * centred, axis=-1, keepdims=True)
    normed = (centred * lax.rsqrt(var + 1e-06) * (1.0 + scale) + shift).astype(jnp.bfloat16)
    down_list = []
    up_list = []
    for which in range(3):
        packed_tensor = jnp.concatenate(
            [adapter_down_factors[0], adapter_up_factors[0][:, which]], axis=1
        )
        packed_tensor = broadcast(packed_tensor, "seq", owner[which])
        down_list.append(packed_tensor[:, :width])
        up_list.append(packed_tensor[:, width:])
    down_factor = jnp.stack(down_list, axis=0)
    up_factor = jnp.stack(up_list, axis=1)
    delta = jnp.einsum("crd,rcn->dcn", down_factor, up_factor, preferred_element_type=jnp.float32)
    merged = (
        lax.all_gather(frozen_query_key_value, "batch", axis=2, tiled=True).astype(jnp.float32)
        + delta
    ).astype(jnp.bfloat16)
    qkv = jnp.einsum("sid,dcn->sicn", normed, merged, preferred_element_type=jnp.float32).astype(
        jnp.bfloat16
    )
    queries = qkv[:, :, 0]
    keys = jnp.concatenate([qkv[:, :, 1], text_key_value[:, 0]], axis=1)
    values = jnp.concatenate([qkv[:, :, 2], text_key_value[:, 1]], axis=1)
    query_heads = queries.reshape(samples, img_rows, heads_here, HEAD_SIZE)
    block = img_rows + txt_rows
    start_top = jnp.full((samples, heads_here, img_rows), -1e30, jnp.float32)
    top = start_top
    key_piece = lax.all_gather(keys, "seq", axis=1, tiled=True)
    value_piece = lax.all_gather(values, "seq", axis=1, tiled=True)
    count = key_piece.shape[1]
    position = jnp.arange(count, dtype=jnp.int32)
    shard = position // block
    inside = position % block
    text_index = shard * txt_rows + inside - img_rows
    live = (inside < img_rows)[None, :] | (text_index[None, :] < prompt_token_length[:, None])
    key_heads = key_piece.reshape(samples, count, heads_here, HEAD_SIZE)
    value_heads = value_piece.reshape(samples, count, heads_here, HEAD_SIZE)
    attention_scores = jnp.einsum(
        "sihe,snhe->shin", query_heads, key_heads, preferred_element_type=jnp.float32
    ) * HEAD_SIZE ** (-0.5)
    attention_scores = jnp.where(live[:, None, None, :], attention_scores, -1e30)
    new_top = jnp.maximum(top, jnp.max(attention_scores, axis=-1))
    expo = jnp.exp(attention_scores - new_top[..., None])
    total = jnp.sum(expo, axis=-1)
    attention_weights = expo.astype(jnp.bfloat16)
    reduced_sum = jnp.einsum(
        "shin,snhe->sihe", attention_weights, value_heads, preferred_element_type=jnp.float32
    )
    top, total, reduced_sum = (new_top, total, reduced_sum)
    attn = (
        (reduced_sum / total.transpose(0, 2, 1)[..., None])
        .reshape(samples, img_rows, resident_columns)
        .astype(jnp.bfloat16)
    )
    proj = jnp.einsum(
        "sin,nd->sid",
        attn,
        lax.all_gather(frozen_output_weight, "batch", axis=0, tiled=True),
        preferred_element_type=jnp.float32,
    )
    summed_heads = lax.psum(proj.astype(jnp.bfloat16), "mp").astype(jnp.float32)
    return (wide + gate * summed_heads).astype(jnp.bfloat16)


def flip(block, axis):
    return lax.ppermute(block, axis, [(0, 1), (1, 0)])


def swap_pair(block, split_axis, concat_axis):
    me = lax.axis_index("batch")
    half = block.shape[split_axis] // 2
    mine = lax.dynamic_slice_in_dim(block, me * half, half, split_axis)
    away = lax.dynamic_slice_in_dim(block, (1 - me) * half, half, split_axis)
    came = flip(away, "batch")
    first = jnp.where(me == 0, mine, came)
    second = jnp.where(me == 0, came, mine)
    return jnp.concatenate([first, second], axis=concat_axis)


def shifted(block, step, count):
    return lax.ppermute(block, "seq", [(i, (i + step) % count) for i in range(count)])


def body_by_sample(
    image_token_states,
    timestep,
    prompt_token_length,
    modulation,
    text_key_value,
    frozen_query_key_value,
    frozen_output_weight,
    adapter_down_factors,
    adapter_up_factors,
    owner,
):
    samples, img_rows, width = image_token_states.shape
    txt_rows = text_key_value.shape[2]
    columns = frozen_query_key_value.shape[2]
    heads_here = columns // HEAD_SIZE
    steps_all = modulation.shape[0]
    at_seq = lax.axis_index("seq")
    at_mp = lax.axis_index("mp")
    at_core = lax.axis_index("batch")
    n_seq = 2 * samples

    up_mine = jnp.zeros(adapter_up_factors.shape[1:2] + adapter_up_factors.shape[3:], jnp.bfloat16)
    for which in range(3):
        up_mine = jnp.where(owner[which] == at_seq, adapter_up_factors[0][:, which], up_mine)
    up_mine = lax.dynamic_slice_in_dim(up_mine, at_core * columns, columns, 1)
    half_rank = up_mine.shape[0] // 2
    down_mine = lax.dynamic_slice_in_dim(adapter_down_factors[0], at_core * half_rank, half_rank, 0)
    packed = jnp.concatenate([down_mine, up_mine[:half_rank], up_mine[half_rank:]], axis=1)
    packed = jnp.stack([packed] + [shifted(packed, k, n_seq) for k in range(1, n_seq)])

    length_row = jnp.broadcast_to(
        prompt_token_length.astype(jnp.bfloat16)[:, None, None, None],
        (samples, 2, 1, text_key_value.shape[3]),
    )
    text = swap_pair(jnp.concatenate([text_key_value, length_row], axis=2), 3, 0)
    text_shape = text.shape
    text = text.reshape(n_seq, -1)
    text_size = text.shape[1]

    away_weight = flip(frozen_output_weight, "mp")

    onehot = (timestep[:, None] == jnp.arange(steps_all, dtype=jnp.int32)[None, :]).astype(
        jnp.float32
    )
    mods = jnp.einsum("st,tcd->scd", onehot, modulation, precision=lax.Precision.HIGHEST)
    shift = mods[:, 0][:, None, :]
    scale = mods[:, 1][:, None, :]
    gate = mods[:, 2][:, None, :]
    wide = image_token_states.astype(jnp.float32)

    rows_mp = img_rows // 2
    part = lax.dynamic_slice_in_dim(image_token_states, at_mp * rows_mp, rows_mp, 1).astype(
        jnp.float32
    )
    mean = jnp.mean(part, axis=-1, keepdims=True)
    centred = part - mean
    var = jnp.mean(centred * centred, axis=-1, keepdims=True)
    normed = (centred * lax.rsqrt(var + 1e-06) * (1.0 + scale) + shift).astype(jnp.bfloat16)

    piece = swap_pair(normed, 1, 0)
    piece_rows = piece.shape[1]
    extra = -(-text_size // width)
    text = jnp.pad(text, ((0, 0), (0, extra * width - text_size))).reshape(n_seq, extra, width)
    piece = jnp.concatenate([piece, text], axis=1)
    blocks = []
    for k in range(n_seq):
        block = lax.dynamic_index_in_dim(piece, (at_seq + k) % n_seq, 0, keepdims=False)
        blocks.append(shifted(block, k, n_seq) if k else block)
    text = [
        block[piece_rows:].reshape(extra * width)[:text_size].reshape(text_shape[1:])
        for block in blocks
    ]
    blocks = [block[:piece_rows] for block in blocks]
    piece = jnp.concatenate(blocks, axis=0)
    piece_mp = jnp.concatenate([flip(block, "mp") for block in blocks], axis=0)
    piece_core = flip(piece, "batch")
    piece_both = flip(piece_mp, "batch")
    merged = []
    chosen = jnp.stack(
        [
            lax.dynamic_index_in_dim(packed, (at_seq - owner[which]) % n_seq, 0, keepdims=False)
            for which in range(3)
        ]
    )
    down_mine = chosen[:, :, :width]
    down_came = flip(down_mine, "batch")
    down_all = jnp.concatenate(
        [
            jnp.where(at_core == 0, down_mine, down_came),
            jnp.where(at_core == 0, down_came, down_mine),
        ],
        axis=1,
    )
    up_all = jnp.concatenate(
        [chosen[:, :, width : width + columns], chosen[:, :, width + columns :]], axis=1
    )
    for which in range(3):
        delta = jnp.einsum(
            "rd,rn->dn", down_all[which], up_all[which], preferred_element_type=jnp.float32
        )
        merged.append(
            (frozen_query_key_value[:, which].astype(jnp.float32) + delta).astype(jnp.bfloat16)
        )
    merged = lax.optimization_barrier(merged)
    early = jnp.concatenate([piece, piece_core], axis=0)
    late = jnp.concatenate([piece_mp, piece_both], axis=0)
    triple = []
    halves = [
        [jnp.dot(rows, m, preferred_element_type=jnp.float32).astype(jnp.bfloat16) for m in merged]
        for rows in (early, late)
    ]
    halves[0] = lax.optimization_barrier(halves[0])
    for which in range(3):
        triple.append(jnp.concatenate([halves[0][which], halves[1][which]], axis=0))
    queries, keys, values = triple
    away_weight, queries = lax.optimization_barrier((away_weight, queries))
    weight_here = lax.all_gather(frozen_output_weight, "batch", axis=0, tiled=True)
    weight_away = lax.all_gather(away_weight, "batch", axis=0, tiled=True)
    tokens = queries.shape[0]
    text_keys = jnp.concatenate([block[0, :txt_rows] for block in text], axis=0)
    text_values = jnp.concatenate([block[1, :txt_rows] for block in text], axis=0)
    length = text[0][0, txt_rows, 0].astype(jnp.int32)
    keys = jnp.concatenate([keys, text_keys], axis=0)
    values = jnp.concatenate([values, text_values], axis=0)
    text_place = (
        (at_seq - jnp.arange(n_seq, dtype=jnp.int32)[:, None]) % n_seq * txt_rows
        + jnp.arange(txt_rows, dtype=jnp.int32)[None, :]
    ).reshape(-1)
    live = jnp.concatenate([jnp.ones((tokens,), bool), text_place < length])
    scores = (
        jnp.einsum(
            "ihe,nhe->hin",
            queries.reshape(-1, heads_here, HEAD_SIZE),
            keys.reshape(-1, heads_here, HEAD_SIZE),
            preferred_element_type=jnp.float32,
        )
        * HEAD_SIZE ** (-0.5)
    )
    scores = jnp.where(live[None, None, :], scores, -1e30)
    top = jnp.max(scores, axis=-1, keepdims=True)
    expo = jnp.exp(scores - top)
    total = jnp.sum(expo, axis=-1)
    summed = jnp.einsum(
        "hin,nhe->ihe",
        expo.astype(jnp.bfloat16),
        values.reshape(-1, heads_here, HEAD_SIZE),
        preferred_element_type=jnp.float32,
    )
    attn = (summed / total.T[:, :, None]).reshape(tokens, columns).astype(jnp.bfloat16)

    attn = attn.reshape(2, 2, n_seq, piece_rows, columns)
    attn = jnp.where(at_mp == 0, attn, attn[::-1])
    attn = jnp.where(at_core == 0, attn, attn[:, ::-1])
    attn = attn.reshape(4, n_seq, piece_rows, columns).transpose(1, 0, 2, 3)
    attn = attn.reshape(n_seq, img_rows, columns)
    back = [shifted(attn[k], -k, n_seq) if k else attn[k] for k in range(n_seq)]
    back_mp = [flip(block, "mp") for block in back]
    back = lax.dynamic_slice_in_dim(jnp.stack(back + back), n_seq - at_seq, n_seq, 0)
    back_mp = lax.dynamic_slice_in_dim(jnp.stack(back_mp + back_mp), n_seq - at_seq, n_seq, 0)
    attn = swap_pair(back, 0, 2)
    attn_away = swap_pair(back_mp, 0, 2)
    proj = jnp.einsum("sin,nd->sid", attn, weight_here, preferred_element_type=jnp.float32)
    proj = lax.optimization_barrier(proj)
    proj = proj + jnp.einsum(
        "sin,nd->sid", attn_away, weight_away, preferred_element_type=jnp.float32
    )
    return (wide + gate * proj).astype(jnp.bfloat16)


def pick(mesh):
    def run(*arrays):
        image, text = arrays[0], arrays[4]
        sizes = mesh.shape
        by_sample = (
            sizes["batch"] == 2
            and sizes["mp"] == 2
            and sizes["seq"] == 2 * image.shape[0]
            and image.shape[1] % 4 == 0
            and arrays[7].shape[1] % 2 == 0
            and sizes["seq"] * text.shape[2] <= 256
        )
        return (body_by_sample if by_sample else body)(*arrays)

    return run


def solution(mesh):
    placed = (
        P(("groups", "batch"), "seq", None),
        P(("groups", "batch")),
        P(("groups", "batch")),
        P(),
        P(("groups", "batch"), None, "seq", "mp"),
        P(None, None, ("mp", "batch")),
        P(("mp", "batch"), None),
        P("seq", None, None),
        P("seq", None, None, "mp"),
        P(),
    )
    return jax.shard_map(
        pick(mesh),
        mesh=mesh,
        in_specs=placed,
        out_specs=P(("groups", "batch"), "seq", None),
        check_vma=False,
    )
```

```python
import jax
import jax.numpy as jnp
from jax import lax
from jax.sharding import PartitionSpec as P

HEAD_SIZE = 64


def broadcast(block, axis, source):
    block = jnp.where(lax.axis_index(axis) == source, block, jnp.zeros_like(block))
    return lax.psum(block, axis)


def body(
    image_token_states,
    timestep,
    prompt_token_length,
    modulation,
    text_key_value,
    frozen_query_key_value,
    frozen_output_weight,
    adapter_down_factors,
    adapter_up_factors,
    owner,
):
    samples, img_rows, width = image_token_states.shape
    txt_rows = text_key_value.shape[2]
    resident_columns = adapter_up_factors.shape[3]
    heads_here = resident_columns // HEAD_SIZE
    steps_all = modulation.shape[0]
    onehot = (timestep[:, None] == jnp.arange(steps_all, dtype=jnp.int32)[None, :]).astype(
        jnp.float32
    )
    mods = jnp.einsum("st,tcd->scd", onehot, modulation, precision=lax.Precision.HIGHEST)
    shift = mods[:, 0][:, None, :]
    scale = mods[:, 1][:, None, :]
    gate = mods[:, 2][:, None, :]
    wide = image_token_states.astype(jnp.float32)
    mean = jnp.mean(wide, axis=-1, keepdims=True)
    centred = wide - mean
    var = jnp.mean(centred * centred, axis=-1, keepdims=True)
    normed = (centred * lax.rsqrt(var + 1e-06) * (1.0 + scale) + shift).astype(jnp.bfloat16)
    down_list = []
    up_list = []
    for which in range(3):
        packed_tensor = jnp.concatenate(
            [adapter_down_factors[0], adapter_up_factors[0][:, which]], axis=1
        )
        packed_tensor = broadcast(packed_tensor, "seq", owner[which])
        down_list.append(packed_tensor[:, :width])
        up_list.append(packed_tensor[:, width:])
    down_factor = jnp.stack(down_list, axis=0)
    up_factor = jnp.stack(up_list, axis=1)
    delta = jnp.einsum("crd,rcn->dcn", down_factor, up_factor, preferred_element_type=jnp.float32)
    merged = (
        lax.all_gather(frozen_query_key_value, "batch", axis=2, tiled=True).astype(jnp.float32)
        + delta
    ).astype(jnp.bfloat16)
    qkv = jnp.einsum("sid,dcn->sicn", normed, merged, preferred_element_type=jnp.float32).astype(
        jnp.bfloat16
    )
    queries = qkv[:, :, 0]
    keys = jnp.concatenate([qkv[:, :, 1], text_key_value[:, 0]], axis=1)
    values = jnp.concatenate([qkv[:, :, 2], text_key_value[:, 1]], axis=1)
    query_heads = queries.reshape(samples, img_rows, heads_here, HEAD_SIZE)
    block = img_rows + txt_rows
    start_top = jnp.full((samples, heads_here, img_rows), -1e30, jnp.float32)
    top = start_top
    key_piece = lax.all_gather(keys, "seq", axis=1, tiled=True)
    value_piece = lax.all_gather(values, "seq", axis=1, tiled=True)
    count = key_piece.shape[1]
    position = jnp.arange(count, dtype=jnp.int32)
    shard = position // block
    inside = position % block
    text_index = shard * txt_rows + inside - img_rows
    live = (inside < img_rows)[None, :] | (text_index[None, :] < prompt_token_length[:, None])
    key_heads = key_piece.reshape(samples, count, heads_here, HEAD_SIZE)
    value_heads = value_piece.reshape(samples, count, heads_here, HEAD_SIZE)
    attention_scores = jnp.einsum(
        "sihe,snhe->shin", query_heads, key_heads, preferred_element_type=jnp.float32
    ) * HEAD_SIZE ** (-0.5)
    attention_scores = jnp.where(live[:, None, None, :], attention_scores, -1e30)
    new_top = jnp.maximum(top, jnp.max(attention_scores, axis=-1))
    expo = jnp.exp(attention_scores - new_top[..., None])
    total = jnp.sum(expo, axis=-1)
    attention_weights = expo.astype(jnp.bfloat16)
    reduced_sum = jnp.einsum(
        "shin,snhe->sihe", attention_weights, value_heads, preferred_element_type=jnp.float32
    )
    top, total, reduced_sum = (new_top, total, reduced_sum)
    attn = (
        (reduced_sum / total.transpose(0, 2, 1)[..., None])
        .reshape(samples, img_rows, resident_columns)
        .astype(jnp.bfloat16)
    )
    proj = jnp.einsum(
        "sin,nd->sid",
        attn,
        lax.all_gather(frozen_output_weight, "batch", axis=0, tiled=True),
        preferred_element_type=jnp.float32,
    )
    summed_heads = lax.psum(proj.astype(jnp.bfloat16), "mp").astype(jnp.float32)
    return (wide + gate * summed_heads).astype(jnp.bfloat16)


def flip(block, axis):
    return lax.ppermute(block, axis, [(0, 1), (1, 0)])


def swap_pair(block, split_axis, concat_axis):
    me = lax.axis_index("batch")
    half = block.shape[split_axis] // 2
    mine = lax.dynamic_slice_in_dim(block, me * half, half, split_axis)
    away = lax.dynamic_slice_in_dim(block, (1 - me) * half, half, split_axis)
    came = flip(away, "batch")
    first = jnp.where(me == 0, mine, came)
    second = jnp.where(me == 0, came, mine)
    return jnp.concatenate([first, second], axis=concat_axis)


def shifted(block, step, count):
    return lax.ppermute(block, "seq", [(i, (i + step) % count) for i in range(count)])


def blocks_of(array, at_seq):
    count = array.shape[0]
    blocks = []
    for k in range(count):
        block = lax.dynamic_index_in_dim(array, (at_seq + k) % count, 0, keepdims=False)
        blocks.append(shifted(block, k, count) if k else block)
    return blocks


def joined(blocks):
    stacked = lax.optimization_barrier(jnp.stack(blocks))
    return stacked.reshape(-1, blocks[0].shape[-1])


def body_by_sample(
    image_token_states,
    timestep,
    prompt_token_length,
    modulation,
    text_key_value,
    frozen_query_key_value,
    frozen_output_weight,
    adapter_down_factors,
    adapter_up_factors,
    owner,
):
    samples, img_rows, width = image_token_states.shape
    txt_rows = text_key_value.shape[2]
    columns = frozen_query_key_value.shape[2]
    heads_here = columns // HEAD_SIZE
    steps_all = modulation.shape[0]
    at_seq = lax.axis_index("seq")
    at_mp = lax.axis_index("mp")
    at_core = lax.axis_index("batch")
    n_seq = 2 * samples

    up_mine = jnp.zeros(adapter_up_factors.shape[1:2] + adapter_up_factors.shape[3:], jnp.bfloat16)
    for which in range(3):
        up_mine = jnp.where(owner[which] == at_seq, adapter_up_factors[0][:, which], up_mine)
    up_mine = lax.dynamic_slice_in_dim(up_mine, at_core * columns, columns, 1)
    half_rank = up_mine.shape[0] // 2
    down_mine = lax.dynamic_slice_in_dim(adapter_down_factors[0], at_core * half_rank, half_rank, 0)
    packed = jnp.concatenate([down_mine, up_mine[:half_rank], up_mine[half_rank:]], axis=1)
    packed = jnp.stack([packed] + [shifted(packed, k, n_seq) for k in range(1, n_seq)])

    length_row = jnp.broadcast_to(
        prompt_token_length.astype(jnp.bfloat16)[:, None, None, None],
        (samples, 2, 1, text_key_value.shape[3]),
    )
    text = swap_pair(jnp.concatenate([text_key_value, length_row], axis=2), 3, 0)

    away_weight = flip(frozen_output_weight, "mp")

    onehot = (timestep[:, None] == jnp.arange(steps_all, dtype=jnp.int32)[None, :]).astype(
        jnp.float32
    )
    mods = jnp.einsum("st,tcd->scd", onehot, modulation, precision=lax.Precision.HIGHEST)
    shift = mods[:, 0][:, None, :]
    scale = mods[:, 1][:, None, :]
    gate = mods[:, 2][:, None, :]
    wide = image_token_states.astype(jnp.float32)

    rows_mp = img_rows // 2
    part = lax.dynamic_slice_in_dim(image_token_states, at_mp * rows_mp, rows_mp, 1).astype(
        jnp.float32
    )
    mean = jnp.mean(part, axis=-1, keepdims=True)
    centred = part - mean
    var = jnp.mean(centred * centred, axis=-1, keepdims=True)
    normed = (centred * lax.rsqrt(var + 1e-06) * (1.0 + scale) + shift).astype(jnp.bfloat16)

    piece = swap_pair(normed, 1, 0)
    piece_rows = piece.shape[1]
    blocks = blocks_of(piece, at_seq)
    text = blocks_of(text, at_seq)
    piece = joined(blocks)
    piece_mp = joined([flip(block, "mp") for block in blocks])
    piece_core = flip(piece, "batch")
    piece_both = flip(piece_mp, "batch")
    merged = []
    chosen = jnp.stack(
        [
            lax.dynamic_index_in_dim(packed, (at_seq - owner[which]) % n_seq, 0, keepdims=False)
            for which in range(3)
        ]
    )
    down_mine = chosen[:, :, :width]
    down_came = flip(down_mine, "batch")
    down_all = jnp.concatenate(
        [
            jnp.where(at_core == 0, down_mine, down_came),
            jnp.where(at_core == 0, down_came, down_mine),
        ],
        axis=1,
    )
    up_all = jnp.concatenate(
        [chosen[:, :, width : width + columns], chosen[:, :, width + columns :]], axis=1
    )
    for which in range(3):
        delta = jnp.einsum(
            "rd,rn->dn", down_all[which], up_all[which], preferred_element_type=jnp.float32
        )
        merged.append(
            (frozen_query_key_value[:, which].astype(jnp.float32) + delta).astype(jnp.bfloat16)
        )
    merged = lax.optimization_barrier(merged)
    early = joined([piece, piece_core])
    late = joined([piece_mp, piece_both])
    triple = []
    halves = [
        [jnp.dot(rows, m, preferred_element_type=jnp.float32).astype(jnp.bfloat16) for m in merged]
        for rows in (early, late)
    ]
    halves[0] = lax.optimization_barrier(halves[0])
    for which in range(3):
        triple.append(jnp.concatenate([halves[0][which], halves[1][which]], axis=0))
    queries, keys, values = triple
    away_weight, queries = lax.optimization_barrier((away_weight, queries))
    weight_here = lax.all_gather(frozen_output_weight, "batch", axis=0, tiled=True)
    weight_away = lax.all_gather(away_weight, "batch", axis=0, tiled=True)
    tokens = queries.shape[0]
    text_keys = jnp.concatenate([block[0, :txt_rows] for block in text], axis=0)
    text_values = jnp.concatenate([block[1, :txt_rows] for block in text], axis=0)
    length = text[0][0, txt_rows, 0].astype(jnp.int32)
    keys = jnp.concatenate([keys, text_keys], axis=0)
    values = jnp.concatenate([values, text_values], axis=0)
    text_place = (
        (at_seq - jnp.arange(n_seq, dtype=jnp.int32)[:, None]) % n_seq * txt_rows
        + jnp.arange(txt_rows, dtype=jnp.int32)[None, :]
    ).reshape(-1)
    live = jnp.concatenate([jnp.ones((tokens,), bool), text_place < length])
    scores = (
        jnp.einsum(
            "ihe,nhe->hin",
            queries.reshape(-1, heads_here, HEAD_SIZE),
            keys.reshape(-1, heads_here, HEAD_SIZE),
            preferred_element_type=jnp.float32,
        )
        * HEAD_SIZE ** (-0.5)
    )
    scores = jnp.where(live[None, None, :], scores, -1e30)
    top = jnp.max(scores, axis=-1, keepdims=True)
    expo = jnp.exp(scores - top)
    total = jnp.sum(expo, axis=-1)
    summed = jnp.einsum(
        "hin,nhe->ihe",
        expo.astype(jnp.bfloat16),
        values.reshape(-1, heads_here, HEAD_SIZE),
        preferred_element_type=jnp.float32,
    )
    attn = (summed / total.T[:, :, None]).reshape(tokens, columns).astype(jnp.bfloat16)

    attn = attn.reshape(2, 2, n_seq, piece_rows, columns)
    attn = jnp.where(at_mp == 0, attn, attn[::-1])
    attn = jnp.where(at_core == 0, attn, attn[:, ::-1])
    attn = attn.reshape(4, n_seq, piece_rows, columns).transpose(1, 0, 2, 3)
    attn = attn.reshape(n_seq, img_rows, columns)
    back = [shifted(attn[k], -k, n_seq) if k else attn[k] for k in range(n_seq)]
    back_mp = [flip(block, "mp") for block in back]
    back = lax.dynamic_slice_in_dim(jnp.stack(back + back), n_seq - at_seq, n_seq, 0)
    back_mp = lax.dynamic_slice_in_dim(jnp.stack(back_mp + back_mp), n_seq - at_seq, n_seq, 0)
    attn = swap_pair(back, 0, 2)
    attn_away = swap_pair(back_mp, 0, 2)
    proj = jnp.einsum("sin,nd->sid", attn, weight_here, preferred_element_type=jnp.float32)
    proj = lax.optimization_barrier(proj)
    proj = proj + jnp.einsum(
        "sin,nd->sid", attn_away, weight_away, preferred_element_type=jnp.float32
    )
    return (wide + gate * proj).astype(jnp.bfloat16)


def pick(mesh):
    def run(*arrays):
        image, text = arrays[0], arrays[4]
        sizes = mesh.shape
        by_sample = (
            sizes["batch"] == 2
            and sizes["mp"] == 2
            and sizes["seq"] == 2 * image.shape[0]
            and image.shape[1] % 4 == 0
            and arrays[7].shape[1] % 2 == 0
            and sizes["seq"] * text.shape[2] <= 256
        )
        return (body_by_sample if by_sample else body)(*arrays)

    return run


def solution(mesh):
    placed = (
        P(("groups", "batch"), "seq", None),
        P(("groups", "batch")),
        P(("groups", "batch")),
        P(),
        P(("groups", "batch"), None, "seq", "mp"),
        P(None, None, ("mp", "batch")),
        P(("mp", "batch"), None),
        P("seq", None, None),
        P("seq", None, None, "mp"),
        P(),
    )
    return jax.shard_map(
        pick(mesh),
        mesh=mesh,
        in_specs=placed,
        out_specs=P(("groups", "batch"), "seq", None),
        check_vma=False,
    )
```

```python
import jax
import jax.numpy as jnp
from jax import lax
from jax.sharding import PartitionSpec as P

HEAD_SIZE = 64


def broadcast(block, axis, source):
    block = jnp.where(lax.axis_index(axis) == source, block, jnp.zeros_like(block))
    return lax.psum(block, axis)


def body(
    image_token_states,
    timestep,
    prompt_token_length,
    modulation,
    text_key_value,
    frozen_query_key_value,
    frozen_output_weight,
    adapter_down_factors,
    adapter_up_factors,
    owner,
):
    samples, img_rows, width = image_token_states.shape
    txt_rows = text_key_value.shape[2]
    resident_columns = adapter_up_factors.shape[3]
    heads_here = resident_columns // HEAD_SIZE
    steps_all = modulation.shape[0]
    onehot = (timestep[:, None] == jnp.arange(steps_all, dtype=jnp.int32)[None, :]).astype(
        jnp.float32
    )
    mods = jnp.einsum("st,tcd->scd", onehot, modulation, precision=lax.Precision.HIGHEST)
    shift = mods[:, 0][:, None, :]
    scale = mods[:, 1][:, None, :]
    gate = mods[:, 2][:, None, :]
    wide = image_token_states.astype(jnp.float32)
    mean = jnp.mean(wide, axis=-1, keepdims=True)
    centred = wide - mean
    var = jnp.mean(centred * centred, axis=-1, keepdims=True)
    normed = (centred * lax.rsqrt(var + 1e-06) * (1.0 + scale) + shift).astype(jnp.bfloat16)
    down_list = []
    up_list = []
    for which in range(3):
        packed_tensor = jnp.concatenate(
            [adapter_down_factors[0], adapter_up_factors[0][:, which]], axis=1
        )
        packed_tensor = broadcast(packed_tensor, "seq", owner[which])
        down_list.append(packed_tensor[:, :width])
        up_list.append(packed_tensor[:, width:])
    down_factor = jnp.stack(down_list, axis=0)
    up_factor = jnp.stack(up_list, axis=1)
    delta = jnp.einsum("crd,rcn->dcn", down_factor, up_factor, preferred_element_type=jnp.float32)
    merged = (
        lax.all_gather(frozen_query_key_value, "batch", axis=2, tiled=True).astype(jnp.float32)
        + delta
    ).astype(jnp.bfloat16)
    qkv = jnp.einsum("sid,dcn->sicn", normed, merged, preferred_element_type=jnp.float32).astype(
        jnp.bfloat16
    )
    queries = qkv[:, :, 0]
    keys = jnp.concatenate([qkv[:, :, 1], text_key_value[:, 0]], axis=1)
    values = jnp.concatenate([qkv[:, :, 2], text_key_value[:, 1]], axis=1)
    query_heads = queries.reshape(samples, img_rows, heads_here, HEAD_SIZE)
    block = img_rows + txt_rows
    start_top = jnp.full((samples, heads_here, img_rows), -1e30, jnp.float32)
    top = start_top
    key_piece = lax.all_gather(keys, "seq", axis=1, tiled=True)
    value_piece = lax.all_gather(values, "seq", axis=1, tiled=True)
    count = key_piece.shape[1]
    position = jnp.arange(count, dtype=jnp.int32)
    shard = position // block
    inside = position % block
    text_index = shard * txt_rows + inside - img_rows
    live = (inside < img_rows)[None, :] | (text_index[None, :] < prompt_token_length[:, None])
    key_heads = key_piece.reshape(samples, count, heads_here, HEAD_SIZE)
    value_heads = value_piece.reshape(samples, count, heads_here, HEAD_SIZE)
    attention_scores = jnp.einsum(
        "sihe,snhe->shin", query_heads, key_heads, preferred_element_type=jnp.float32
    ) * HEAD_SIZE ** (-0.5)
    attention_scores = jnp.where(live[:, None, None, :], attention_scores, -1e30)
    new_top = jnp.maximum(top, jnp.max(attention_scores, axis=-1))
    expo = jnp.exp(attention_scores - new_top[..., None])
    total = jnp.sum(expo, axis=-1)
    attention_weights = expo.astype(jnp.bfloat16)
    reduced_sum = jnp.einsum(
        "shin,snhe->sihe", attention_weights, value_heads, preferred_element_type=jnp.float32
    )
    top, total, reduced_sum = (new_top, total, reduced_sum)
    attn = (
        (reduced_sum / total.transpose(0, 2, 1)[..., None])
        .reshape(samples, img_rows, resident_columns)
        .astype(jnp.bfloat16)
    )
    proj = jnp.einsum(
        "sin,nd->sid",
        attn,
        lax.all_gather(frozen_output_weight, "batch", axis=0, tiled=True),
        preferred_element_type=jnp.float32,
    )
    summed_heads = lax.psum(proj.astype(jnp.bfloat16), "mp").astype(jnp.float32)
    return (wide + gate * summed_heads).astype(jnp.bfloat16)


def flip(block, axis):
    return lax.ppermute(block, axis, [(0, 1), (1, 0)])


def swap_pair(block, split_axis, concat_axis):
    me = lax.axis_index("batch")
    half = block.shape[split_axis] // 2
    mine = lax.dynamic_slice_in_dim(block, me * half, half, split_axis)
    away = lax.dynamic_slice_in_dim(block, (1 - me) * half, half, split_axis)
    came = flip(away, "batch")
    first = jnp.where(me == 0, mine, came)
    second = jnp.where(me == 0, came, mine)
    return jnp.concatenate([first, second], axis=concat_axis)


def shifted(block, step, count):
    return lax.ppermute(block, "seq", [(i, (i + step) % count) for i in range(count)])


def body_by_sample(
    image_token_states,
    timestep,
    prompt_token_length,
    modulation,
    text_key_value,
    frozen_query_key_value,
    frozen_output_weight,
    adapter_down_factors,
    adapter_up_factors,
    owner,
):
    samples, img_rows, width = image_token_states.shape
    txt_rows = text_key_value.shape[2]
    columns = frozen_query_key_value.shape[2]
    heads_here = columns // HEAD_SIZE
    steps_all = modulation.shape[0]
    at_seq = lax.axis_index("seq")
    at_mp = lax.axis_index("mp")
    at_core = lax.axis_index("batch")
    n_seq = 2 * samples

    up_mine = jnp.zeros(adapter_up_factors.shape[1:2] + adapter_up_factors.shape[3:], jnp.bfloat16)
    for which in range(3):
        up_mine = jnp.where(owner[which] == at_seq, adapter_up_factors[0][:, which], up_mine)
    up_mine = lax.dynamic_slice_in_dim(up_mine, at_core * columns, columns, 1)
    half_rank = up_mine.shape[0] // 2
    down_mine = lax.dynamic_slice_in_dim(adapter_down_factors[0], at_core * half_rank, half_rank, 0)
    packed = jnp.concatenate([down_mine, up_mine[:half_rank], up_mine[half_rank:]], axis=1)
    packed = jnp.stack([packed] + [shifted(packed, k, n_seq) for k in range(1, n_seq)])

    length_row = jnp.broadcast_to(
        prompt_token_length.astype(jnp.bfloat16)[:, None, None, None],
        (samples, 2, 1, text_key_value.shape[3]),
    )
    text = swap_pair(jnp.concatenate([text_key_value, length_row], axis=2), 3, 0)
    text_shape = text.shape
    text = text.reshape(n_seq, -1)
    text_size = text.shape[1]

    away_weight = flip(frozen_output_weight, "mp")

    onehot = (timestep[:, None] == jnp.arange(steps_all, dtype=jnp.int32)[None, :]).astype(
        jnp.float32
    )
    mods = jnp.einsum("st,tcd->scd", onehot, modulation, precision=lax.Precision.HIGHEST)
    shift = mods[:, 0][:, None, :]
    scale = mods[:, 1][:, None, :]
    gate = mods[:, 2][:, None, :]
    wide = image_token_states.astype(jnp.float32)

    rows_mp = img_rows // 2
    part = lax.dynamic_slice_in_dim(image_token_states, at_mp * rows_mp, rows_mp, 1).astype(
        jnp.float32
    )
    mean = jnp.mean(part, axis=-1, keepdims=True)
    centred = part - mean
    var = jnp.mean(centred * centred, axis=-1, keepdims=True)
    normed = (centred * lax.rsqrt(var + 1e-06) * (1.0 + scale) + shift).astype(jnp.bfloat16)

    piece = swap_pair(normed, 1, 0)
    piece_rows = piece.shape[1]
    extra = -(-text_size // width)
    text = jnp.pad(text, ((0, 0), (0, extra * width - text_size))).reshape(n_seq, extra, width)
    piece = jnp.concatenate([piece, text], axis=1)
    piece = lax.all_to_all(piece, "seq", 0, 0, tiled=True)
    text = piece[:, piece_rows:].reshape(n_seq, extra * width)[:, :text_size].reshape(text_shape)
    piece = piece[:, :piece_rows]
    piece = piece.reshape(n_seq * piece_rows, width)
    piece_mp = flip(piece, "mp")
    piece_core = flip(piece, "batch")
    piece_both = flip(piece_mp, "batch")
    merged = []
    chosen = jnp.stack(
        [
            lax.dynamic_index_in_dim(packed, (at_seq - owner[which]) % n_seq, 0, keepdims=False)
            for which in range(3)
        ]
    )
    down_mine = chosen[:, :, :width]
    down_came = flip(down_mine, "batch")
    down_all = jnp.concatenate(
        [
            jnp.where(at_core == 0, down_mine, down_came),
            jnp.where(at_core == 0, down_came, down_mine),
        ],
        axis=1,
    )
    up_all = jnp.concatenate(
        [chosen[:, :, width : width + columns], chosen[:, :, width + columns :]], axis=1
    )
    for which in range(3):
        delta = jnp.einsum(
            "rd,rn->dn", down_all[which], up_all[which], preferred_element_type=jnp.float32
        )
        merged.append(
            (frozen_query_key_value[:, which].astype(jnp.float32) + delta).astype(jnp.bfloat16)
        )
    merged = lax.optimization_barrier(merged)
    early = jnp.concatenate([piece, piece_core], axis=0)
    late = jnp.concatenate([piece_mp, piece_both], axis=0)
    triple = []
    halves = [
        [jnp.dot(rows, m, preferred_element_type=jnp.float32).astype(jnp.bfloat16) for m in merged]
        for rows in (early, late)
    ]
    halves[0] = lax.optimization_barrier(halves[0])
    for which in range(3):
        triple.append(jnp.concatenate([halves[0][which], halves[1][which]], axis=0))
    queries, keys, values = triple
    away_weight, queries = lax.optimization_barrier((away_weight, queries))
    weight_here = lax.all_gather(frozen_output_weight, "batch", axis=0, tiled=True)
    weight_away = lax.all_gather(away_weight, "batch", axis=0, tiled=True)
    tokens = queries.shape[0]
    text_keys = text[:, 0, :txt_rows].reshape(n_seq * txt_rows, columns)
    text_values = text[:, 1, :txt_rows].reshape(n_seq * txt_rows, columns)
    length = text[0, 0, txt_rows, 0].astype(jnp.int32)
    keys = jnp.concatenate([keys, text_keys], axis=0)
    values = jnp.concatenate([values, text_values], axis=0)
    position = jnp.arange(keys.shape[0], dtype=jnp.int32)
    live = position < tokens + length
    scores = (
        jnp.einsum(
            "ihe,nhe->hin",
            queries.reshape(-1, heads_here, HEAD_SIZE),
            keys.reshape(-1, heads_here, HEAD_SIZE),
            preferred_element_type=jnp.float32,
        )
        * HEAD_SIZE ** (-0.5)
    )
    scores = jnp.where(live[None, None, :], scores, -1e30)
    top = jnp.max(scores, axis=-1, keepdims=True)
    expo = jnp.exp(scores - top)
    total = jnp.sum(expo, axis=-1)
    summed = jnp.einsum(
        "hin,nhe->ihe",
        expo.astype(jnp.bfloat16),
        values.reshape(-1, heads_here, HEAD_SIZE),
        preferred_element_type=jnp.float32,
    )
    attn = (summed / total.T[:, :, None]).reshape(tokens, columns).astype(jnp.bfloat16)

    attn = attn.reshape(2, 2, n_seq, piece_rows, columns)
    attn = jnp.where(at_mp == 0, attn, attn[::-1])
    attn = jnp.where(at_core == 0, attn, attn[:, ::-1])
    attn = attn.reshape(4, n_seq, piece_rows, columns).transpose(1, 0, 2, 3)
    attn = lax.all_to_all(attn.reshape(n_seq, img_rows, columns), "seq", 0, 0, tiled=True)
    attn = swap_pair(attn, 0, 2)
    attn_away = flip(attn, "mp")
    proj = jnp.einsum("sin,nd->sid", attn, weight_here, preferred_element_type=jnp.float32)
    proj = lax.optimization_barrier(proj)
    proj = proj + jnp.einsum(
        "sin,nd->sid", attn_away, weight_away, preferred_element_type=jnp.float32
    )
    return (wide + gate * proj).astype(jnp.bfloat16)


def pick(mesh):
    def run(*arrays):
        image, text = arrays[0], arrays[4]
        sizes = mesh.shape
        by_sample = (
            sizes["batch"] == 2
            and sizes["mp"] == 2
            and sizes["seq"] == 2 * image.shape[0]
            and image.shape[1] % 4 == 0
            and arrays[7].shape[1] % 2 == 0
            and sizes["seq"] * text.shape[2] <= 256
        )
        return (body_by_sample if by_sample else body)(*arrays)

    return run


def solution(mesh):
    placed = (
        P(("groups", "batch"), "seq", None),
        P(("groups", "batch")),
        P(("groups", "batch")),
        P(),
        P(("groups", "batch"), None, "seq", "mp"),
        P(None, None, ("mp", "batch")),
        P(("mp", "batch"), None),
        P("seq", None, None),
        P("seq", None, None, "mp"),
        P(),
    )
    return jax.shard_map(
        pick(mesh),
        mesh=mesh,
        in_specs=placed,
        out_specs=P(("groups", "batch"), "seq", None),
        check_vma=False,
    )
```
